256 devices in a mesh: seg: 32 (over y, x, core), ctx: 8 (over z).
Axes of the slice: x: 4, y: 4, z: 8, core: 2. Of those that a mesh axis runs over, the one named last changes fastest.
Arguments:
- token_ids: int32 [65536], P(('seg', 'ctx')), may hold values from 65 to 116, as said below
- query_in: bfloat16 [65536, 2048], P(('seg', 'ctx')), may hold values from -6 to 6
- key_in: bfloat16 [65536, 2048], P(('seg', 'ctx')), may hold values from -6 to 6
- value_in: bfloat16 [65536, 2048], P(('seg', 'ctx')), may hold values from -6 to 6
- short_filters: float32 [3, 7, 2048], replicated, may hold values from -2 to 2
- long_filter: bfloat16 [128, 128], replicated, may hold values from -0.6 to 0.6
- skip_gain: float32 [2048], replicated, may hold values from 0.5 to 1.5
- out_grad: bfloat16 [65536, 2048], P(('seg', 'ctx')), may hold values from -9 to 9
Outputs:
- block_out: bfloat16 [65536, 2048], P(('seg', 'ctx'))
- grad_query: bfloat16 [65536, 2048], P(('seg', 'ctx'))
- grad_key: bfloat16 [65536, 2048], P(('seg', 'ctx'))
- grad_value: bfloat16 [65536, 2048], P(('seg', 'ctx'))
- grad_long: float32 [128, 128], replicated
- grad_skip: float32 [2048], replicated
- grad_short: float32 [3, 7, 2048], replicated
The draws below stay inside these ranges and needn't reach their ends.
Inputs may be any that keep to these rules, and one draw needn't show every extreme that they name: `token_ids`: every id is one of the byte codes 65 67 71 84 78 (A C G T N) or 97 99 103 116 110 (the same in lowercase, marking repeats). Case comes in aligned runs of 32 positions, except that the first position is always 65 and the last always 116, whatever the case of their runs.
All inputs are finite; a program needn't handle non-finite values.
Results may differ from the reference program's by a relative error of at most 0.011.
Values may be sent and summed in bfloat16 or wider, within the bound.
No kernel may reach another device: no remote copies, remote signals or barrier semaphores. Data moves between devices by JAX's collectives and lax.ppermute only.
A program may use at most 192 MiB of HBM per device.

```python
import jax
import jax.numpy as jnp
from jax import lax

C = 2048
GROUP = 16
TAPS = 128
SHORT = 7
G = 128
TOKENS = 65536


def draw_token_ids(key, part):
    key = jax.random.fold_in(key, 5)
    base_key, case_key = jax.random.split(key)
    letters = jnp.array([65, 67, 71, 84, 78, 97, 99, 103, 116, 110], jnp.int32)
    base = jax.random.randint(base_key, (TOKENS,), 0, 5)
    runs = jax.random.randint(case_key, (TOKENS // 32,), 0, 2)
    lowered = jnp.repeat(runs, 32)
    chosen = letters[base + 5 * lowered]
    chosen = chosen.at[0].set(65)
    return chosen.at[TOKENS - 1].set(116)


def draw_long_filter(key, part):
    key = jax.random.fold_in(key, 11)
    noise_key, rate_key = jax.random.split(key)
    noise = jnp.clip(jax.random.normal(noise_key, (G, TAPS), jnp.float32), -4.0, 4.0)
    rates = jnp.exp(jax.random.uniform(rate_key, (G,), jnp.float32, jnp.log(0.002), jnp.log(0.05)))
    envelope = jnp.exp(-rates[:, None] * jnp.arange(TAPS, dtype=jnp.float32)[None, :])
    return (0.15 * noise * envelope).astype(jnp.bfloat16)


def draw_out_grad(key, part):
    key = jax.random.fold_in(key, 17)
    position = jnp.arange(TOKENS, dtype=jnp.float32)[:, None] / TOKENS
    noise = jnp.clip(jax.random.normal(key, (TOKENS, C), jnp.float32), -6.0, 6.0)
    rising = 0.5 + position
    return (noise * rising).astype(jnp.bfloat16)


def shard_levels(own_key, shape, pieces, least, high):
    loudness, own = 1.0, jax.random.fold_in(own_key, 6)
    for axis_at, blocks in pieces:
        heights = jnp.exp(jax.random.uniform(jax.random.fold_in(own, axis_at), (blocks,), jnp.float32, least / len(pieces), high / len(pieces)))
        loudness = loudness * jnp.repeat(heights, shape[axis_at] // blocks).reshape([-1 if axis == axis_at else 1 for axis in range(len(shape))])
    return loudness


def normal_values(key, shape, width, most, pieces=(), kind=jnp.bfloat16):
    factor_of = shard_levels(key, shape, pieces, -0.22, 0.18) if pieces else 1.0
    drawn = jax.random.normal(key, shape, jnp.float32) * width * factor_of
    return jnp.minimum(jnp.maximum(drawn, -most), most).astype(kind)


def setup_inputs(seed: int = 0) -> dict:
    key_of = jax.random.split(jax.random.key(seed), 9)
    return {
        "token_ids": draw_token_ids(jax.random.fold_in(key_of[8], 71), 0),
        "query_in": normal_values(key_of[1], (TOKENS, C), 1.0, 6.0, ((0, 256),)),
        "key_in": normal_values(key_of[2], (TOKENS, C), 1.0, 6.0, ((0, 256),)),
        "value_in": normal_values(key_of[3], (TOKENS, C), 1.0, 6.0, ((0, 256),)),
        "short_filters": normal_values(key_of[4], (3, SHORT, C), SHORT ** -0.5, 2.0, (), jnp.float32),
        "long_filter": draw_long_filter(jax.random.fold_in(key_of[8], 71), 0),
        "skip_gain": jnp.clip(jax.random.uniform(key_of[6], (C,), jnp.float32, 0.5, 1.5), 0.5, 1.5),
        "out_grad": draw_out_grad(jax.random.fold_in(key_of[8], 71), 0),
    }


def featurize(framed, weights):
    margin = weights.shape[0] - 1
    length = framed.shape[0] - margin
    running = jnp.zeros((length, framed.shape[1]), jnp.float32)
    for offset in range(margin + 1):
        running = running + weights[offset][None, :] * framed[margin - offset:margin - offset + length].astype(jnp.float32)
    return running

def featurize_back(framed, weights):
    margin = weights.shape[0] - 1
    length = framed.shape[0] - margin
    running = jnp.zeros((length, framed.shape[1]), jnp.float32)
    for offset in range(margin + 1):
        running = running + weights[offset][None, :] * framed[offset:offset + length].astype(jnp.float32)
    return running

def short_grad(grad_act, framed, margin):
    length = grad_act.shape[0]
    parts = [lax.optimization_barrier(jnp.sum(grad_act.astype(jnp.float32) * framed[margin - offset:margin - offset + length].astype(jnp.float32), axis=0)) for offset in range(margin + 1)]
    return jnp.stack(parts)

def forward_table(long_filter):
    groups = long_filter.shape[0]
    pattern = jnp.concatenate([jnp.zeros((groups, 1), long_filter.dtype), long_filter[:, ::-1], jnp.zeros((groups, TAPS), long_filter.dtype)], axis=1)
    tiled = jnp.tile(pattern, (1, TAPS))[:, :TAPS * 2 * TAPS]
    return tiled.reshape(groups, TAPS, 2 * TAPS)

def backward_table(long_filter):
    groups = long_filter.shape[0]
    pattern = jnp.concatenate([long_filter, jnp.zeros((groups, TAPS + 1), long_filter.dtype)], axis=1)
    tiled = jnp.tile(pattern, (1, TAPS))[:, :TAPS * 2 * TAPS]
    return tiled.reshape(groups, TAPS, 2 * TAPS)

def make_windows(framed, groups):
    count = framed.shape[0] // TAPS - 1
    blocks = framed.reshape(count + 1, TAPS, framed.shape[1])
    joined = jnp.concatenate([blocks[:-1], blocks[1:]], axis=1)
    return joined.reshape(count, 2 * TAPS, groups, framed.shape[1] // groups)

def apply_table(toeplitz, windows_x):
    count = windows_x.shape[0]
    result = jnp.einsum('gts,bsgk->btgk', toeplitz.astype(jnp.float32), windows_x.astype(jnp.float32), precision=lax.Precision.HIGHEST)
    return result.reshape(count * TAPS, -1)

def skew_sum(products):
    groups = products.shape[0]
    flattened = products.reshape(groups, TAPS * 2 * TAPS)
    extended = jnp.concatenate([flattened, jnp.zeros((groups, TAPS), jnp.float32)], axis=1)
    extended = extended.reshape(groups, TAPS, 2 * TAPS + 1)
    return lax.optimization_barrier(jnp.sum(extended, axis=1))[:, TAPS:0:-1]

def reference(token_ids, query_in, key_in, value_in, short_filters, long_filter, skip_gain, out_grad):
    channels = query_in.shape[1]
    groups = channels // GROUP
    margin = SHORT - 1
    lead_rows = jnp.zeros((margin, channels), jnp.bfloat16)
    framed_q = jnp.concatenate([lead_rows, query_in], axis=0)
    framed_k = jnp.concatenate([lead_rows, key_in], axis=0)
    framed_v = jnp.concatenate([lead_rows, value_in], axis=0)
    query_act = featurize(framed_q, short_filters[0])
    key_act = featurize(framed_k, short_filters[1])
    value_act = featurize(framed_v, short_filters[2])
    gated = (key_act * value_act).astype(jnp.bfloat16)
    framed_x = jnp.concatenate([jnp.zeros((TAPS, channels), jnp.bfloat16), gated], axis=0)
    windows_x = make_windows(framed_x, groups)
    filtered = apply_table(forward_table(long_filter), windows_x) + skip_gain[None, :] * gated.astype(jnp.float32)
    block_out = (query_act * filtered).astype(jnp.bfloat16)
    loss_weight = jnp.where(token_ids >= 97, 0.1, 1.0).astype(jnp.float32)
    grad_out = out_grad.astype(jnp.float32) * loss_weight[:, None]
    grad_scaled = (grad_out * query_act).astype(jnp.bfloat16)
    grad_act_query = (grad_out * filtered).astype(jnp.bfloat16)
    framed_g = jnp.concatenate([grad_scaled, jnp.zeros((TAPS, channels), jnp.bfloat16)], axis=0)
    grad_gated = skip_gain[None, :] * grad_scaled.astype(jnp.float32) + apply_table(backward_table(long_filter), make_windows(framed_g, groups))
    grad_act_key = (grad_gated * value_act).astype(jnp.bfloat16)
    grad_act_value = (grad_gated * key_act).astype(jnp.bfloat16)
    trail_rows = jnp.zeros((margin, channels), jnp.bfloat16)
    grad_query = featurize_back(jnp.concatenate([grad_act_query, trail_rows], axis=0), short_filters[0]).astype(jnp.bfloat16)
    grad_key = featurize_back(jnp.concatenate([grad_act_key, trail_rows], axis=0), short_filters[1]).astype(jnp.bfloat16)
    grad_value = featurize_back(jnp.concatenate([grad_act_value, trail_rows], axis=0), short_filters[2]).astype(jnp.bfloat16)
    count = windows_x.shape[0]
    grad_blocks = grad_scaled.reshape(count, TAPS, groups, GROUP)
    products = jnp.einsum('btgk,bsgk->gts', grad_blocks.astype(jnp.float32), windows_x.astype(jnp.float32), precision=lax.Precision.HIGHEST)
    norm_scale = float(TOKENS) ** (-0.5)
    grad_long = skew_sum(products) * norm_scale
    grad_skip = lax.optimization_barrier(jnp.sum(grad_scaled.astype(jnp.float32) * gated.astype(jnp.float32), axis=0)) * norm_scale
    grad_short = jnp.stack([short_grad(grad_act_query, framed_q, margin), short_grad(grad_act_key, framed_k, margin), short_grad(grad_act_value, framed_v, margin)]) * norm_scale
    return (block_out, grad_query, grad_key, grad_value, grad_long, grad_skip, grad_short)
```

```python
import functools

import jax
import jax.numpy as jnp
from jax import lax
from jax.experimental import pallas as pl
from jax.experimental.pallas import tpu as pltpu
from jax.sharding import PartitionSpec as P

GROUP = 16
TAPS = 128
SHORT = 7
LANES = 128
PER_TILE = LANES // GROUP
EDGE = 16
RUN = 32
PART_ROWS = 32
AXES = ("seg", "ctx")
MIB = 1024 * 1024
F32 = jnp.float32
BF16 = jnp.bfloat16


def causal(frame, which, taps, start, count):
    total = taps[which, 0:1] * frame[pl.ds(start, count)]
    for j in range(1, SHORT):
        total = total + taps[which, j : j + 1] * frame[pl.ds(start - j, count)]
    return total


def weight_of(repeat):
    return jnp.where(repeat > 0.5, F32(0.1), F32(1.0))


def mark_repeats(ids, marks):
    rows = marks.shape[0]
    row = lax.broadcasted_iota(jnp.int32, (RUN, LANES), 0)

    def mark(at):
        return jnp.full((RUN, LANES), (ids[at] >= 97).astype(F32))

    for r in range(0, rows, RUN):
        run = mark(r + 1)
        if r == 0:
            run = jnp.where(row == 0, mark(0), run)
        if r + RUN == rows:
            run = jnp.where(row == RUN - 1, mark(rows - 1), run)
        marks[r : r + RUN] = run


def edges_kernel(
    ids, q, g, k_edge, k, v_edge, v, q_tail, taps_ref, right, left, kf, vf, qf, rep
):
    @pl.when(pl.program_id(0) == 0)
    def _():
        mark_repeats(ids, rep)

    for lt in range(q.shape[1] // LANES):
        ls = slice(lt * LANES, (lt + 1) * LANES)
        taps = taps_ref[:, :, ls]
        kf[:EDGE] = k_edge[:, ls].astype(F32)
        vf[:EDGE] = v_edge[:, ls].astype(F32)
        kf[EDGE:] = k[:, ls].astype(F32)
        vf[EDGE:] = v[:, ls].astype(F32)
        qf[...] = q[:, ls].astype(F32)
        for r in range(0, TAPS, 64):
            act_k = causal(kf, 1, taps, EDGE + r, 64)
            act_v = causal(vf, 2, taps, EDGE + r, 64)
            right[r : r + 64, ls] = (act_k * act_v).astype(BF16)
        right[TAPS : TAPS + EDGE, ls] = k[TAPS - EDGE :, ls]
        right[TAPS + EDGE : TAPS + 2 * EDGE, ls] = v[TAPS - EDGE :, ls]
        right[TAPS + 2 * EDGE : TAPS + 3 * EDGE, ls] = q_tail[:, ls]
        for r, count in ((EDGE, 48), (EDGE + 48, 64)):
            act_q = causal(qf, 0, taps, r, count)
            grad = g[r : r + count, ls].astype(F32) * weight_of(rep[r : r + count])
            left[r - EDGE : r - EDGE + count, ls] = (grad * act_q).astype(BF16)
        left[TAPS - EDGE : TAPS, ls] = q[:EDGE, ls]
        left[TAPS : TAPS + EDGE, ls] = g[:EDGE, ls]
        left[TAPS + EDGE : TAPS + 2 * EDGE, ls] = rep[:EDGE].astype(BF16)


def tables_kernel(taps, fwd, bwd, plain, backwards):
    row = lax.broadcasted_iota(jnp.int32, (TAPS, TAPS), 0)
    col = lax.broadcasted_iota(jnp.int32, (TAPS, TAPS), 1)
    tile = pl.program_id(0)

    @pl.when(tile == 0)
    def _():
        mirror = ((row + col == TAPS) | ((row == 0) & (col == 0))).astype(BF16)
        plain[...] = taps[...].astype(F32)
        backwards[...] = jnp.dot(taps[...], mirror, preferred_element_type=F32)

    first = pl.multiple_of(tile * PER_TILE, PER_TILE)
    plain_rows = plain[pl.ds(first, PER_TILE)]
    backward_rows = backwards[pl.ds(first, PER_TILE)]

    def rings(source, g):
        spread = jnp.broadcast_to(source[g : g + 1], (TAPS, TAPS))
        return pltpu.roll(spread, 0, 1, stride=1, stride_axis=0)

    for g in range(PER_TILE):
        ring = rings(backward_rows, g)
        fwd[g, :, :TAPS] = jnp.where(col > row, ring, 0.0).astype(BF16)
        fwd[g, :, TAPS:] = jnp.where(col <= row, ring, 0.0).astype(BF16)
        ring = rings(plain_rows, g)
        bwd[g, :, :TAPS] = jnp.where(col >= row, ring, 0.0).astype(BF16)
        bwd[g, :, TAPS:] = jnp.where(col < row, ring, 0.0).astype(BF16)


def main_kernel(
    ids, q, k, v, g, taps_ref, skip_ref, fwd, bwd, from_left, from_right,
    out, gq, gk, gv, heads, part,
    qf, kf, vf, xs, gs, act_q, act_k, act_v, prod_p, prod_f, prod_b, diag, rep,
):
    tile = pl.program_id(0)

    @pl.when(tile == 0)
    def _():
        mark_repeats(ids, rep)

    rows = q.shape[0]
    step = 64
    taps = taps_ref[...]
    skip = skip_ref[...]
    qf[EDGE : EDGE + rows] = q[...].astype(F32)
    kf[EDGE : EDGE + rows] = k[...].astype(F32)
    vf[EDGE : EDGE + rows] = v[...].astype(F32)
    kf[:EDGE] = from_left[TAPS : TAPS + EDGE].astype(F32)
    vf[:EDGE] = from_left[TAPS + EDGE : TAPS + 2 * EDGE].astype(F32)
    qf[:EDGE] = from_left[TAPS + 2 * EDGE : TAPS + 3 * EDGE].astype(F32)
    qf[EDGE + rows :] = from_right[TAPS - EDGE : TAPS].astype(F32)
    xs[:TAPS] = from_left[:TAPS]
    gs[rows + EDGE :] = from_right[: TAPS - EDGE]

    skip_sum = jnp.zeros((8, LANES), F32)
    for r in range(0, rows, step):
        a_q = causal(qf, 0, taps, EDGE + r, step)
        a_k = causal(kf, 1, taps, EDGE + r, step)
        a_v = causal(vf, 2, taps, EDGE + r, step)
        act_q[r : r + step] = a_q
        act_k[r : r + step] = a_k
        act_v[r : r + step] = a_v
        gated = (a_k * a_v).astype(BF16)
        xs[TAPS + r : TAPS + r + step] = gated
        grad = g[r : r + step].astype(F32) * weight_of(rep[r : r + step])
        scaled = (grad * a_q).astype(BF16)
        gs[r : r + step] = scaled
        both = scaled.astype(F32) * gated.astype(F32)
        skip_sum = skip_sum + jnp.sum(both.reshape(step // 8, 8, LANES), axis=0)
    a_q = causal(qf, 0, taps, EDGE + rows, EDGE)
    grad = from_right[TAPS : TAPS + EDGE].astype(F32) * weight_of(
        from_right[TAPS + EDGE : TAPS + 2 * EDGE].astype(F32)
    )
    gs[rows : rows + EDGE] = (grad * a_q).astype(BF16)

    lane_group = lax.broadcasted_iota(jnp.int32, (8, LANES), 1) // GROUP
    group2 = jnp.concatenate([lane_group, lane_group], axis=1)
    win_g = jnp.concatenate([gs[: 2 * TAPS], gs[TAPS:]], axis=1)
    own_x = jnp.concatenate([xs[TAPS : 2 * TAPS], xs[2 * TAPS :]], axis=1)

    def spread(table, windows, prod):
        prod[...] = jnp.dot(
            table[...].reshape(PER_TILE * TAPS, 2 * TAPS), windows, preferred_element_type=F32
        )

    def gather(prod, r, count):
        block, at = divmod(r, TAPS)
        ls = slice(block * LANES, (block + 1) * LANES)
        picks = jnp.broadcast_to(lane_group[0:1], (count, LANES))
        total = prod[at : at + count, ls]
        for n in range(1, PER_TILE):
            total = jnp.where(picks == n, prod[n * TAPS + at : n * TAPS + at + count, ls], total)
        return total

    def short_sums(sums, grads, frame, r):
        wide_grads = grads.astype(F32)
        return [
            total
            + jnp.sum(
                (wide_grads * frame[pl.ds(EDGE + r - j, step)]).reshape(step // 8, 8, LANES),
                axis=0,
            )
            for j, total in enumerate(sums)
        ]

    zeros = [jnp.zeros((8, LANES), F32)] * SHORT
    sums_q, sums_k, sums_v = zeros, zeros, zeros
    win_x = jnp.concatenate([xs[: 2 * TAPS], xs[TAPS:]], axis=1)
    spread(fwd, win_x, prod_f)
    spread(bwd, win_g, prod_b)
    wide = jnp.broadcast_to(group2[0:1], (TAPS, 2 * LANES))
    masked = jnp.concatenate(
        [jnp.where(wide == n, own_x, jnp.zeros_like(own_x)) for n in range(PER_TILE)], axis=0
    )
    prod_p[...] = lax.dot_general(
        masked, win_g, (((1,), (1,)), ((), ())), preferred_element_type=F32
    )
    for r in range(0, rows, step):
        filtered = gather(prod_f, r, step) + skip * xs[TAPS + r : TAPS + r + step].astype(F32)
        out[r : r + step] = (act_q[r : r + step] * filtered).astype(BF16)
        grad = g[r : r + step].astype(F32) * weight_of(rep[r : r + step])
        grads = (grad * filtered).astype(BF16)
        gq[r : r + step] = grads
        sums_q = short_sums(sums_q, grads, qf, r)
    for r in range(0, rows, step):
        grad_gated = skip * gs[r : r + step].astype(F32) + gather(prod_b, r, step)
        grads = (grad_gated * act_v[r : r + step]).astype(BF16)
        gk[r : r + step] = grads
        sums_k = short_sums(sums_k, grads, kf, r)
        grads = (grad_gated * act_k[r : r + step]).astype(BF16)
        gv[r : r + step] = grads
        sums_v = short_sums(sums_v, grads, vf, r)
    sub = lax.broadcasted_iota(jnp.int32, (8, LANES), 0)
    lane = lax.broadcasted_iota(jnp.int32, (8, LANES), 1)
    for n in range(PER_TILE):
        total = jnp.zeros((8, LANES), F32)
        for m in range(TAPS // 8):
            r = n * TAPS + m * 8
            ring = jnp.where(
                lane >= sub + m * 8, prod_p[r : r + 8, :LANES], prod_p[r : r + 8, LANES:]
            )
            total = total + (pltpu.roll(ring, LANES - 8 * m, 1) if m else ring)
        diag[n * 8 : n * 8 + 8] = total
    long_part = diag[pl.ds(0, PER_TILE, stride=8)]
    for r in range(1, 8):
        long_part = long_part + pltpu.roll(diag[pl.ds(r, PER_TILE, stride=8)], LANES - r, 1)
    part[0, :PER_TILE] = long_part

    heads[:EDGE] = gq[:EDGE]
    heads[EDGE : 2 * EDGE] = gk[:EDGE]
    heads[2 * EDGE :] = gv[:EDGE]
    lines = [jnp.sum(s, axis=0, keepdims=True) for s in sums_q + sums_k + sums_v + [skip_sum]]
    lines.append(jnp.zeros((PART_ROWS - PER_TILE - len(lines), LANES), F32))
    part[0, PER_TILE:] = jnp.concatenate(lines, axis=0)


def back_kernel(grads, heads, taps_ref, result, frame):
    rows = grads.shape[0]
    step = 64
    for lt in range(grads.shape[1] // LANES):
        ls = slice(lt * LANES, (lt + 1) * LANES)
        frame[:rows] = grads[:, ls].astype(F32)
        frame[rows:] = heads[:, ls].astype(F32)
        for r in range(0, rows, step):
            total = taps_ref[0, 0:1, ls] * frame[pl.ds(r, step)]
            for j in range(1, SHORT):
                total = total + taps_ref[0, j : j + 1, ls] * frame[pl.ds(r + j, step)]
            result[r : r + step, ls] = total.astype(BF16)


def params(limit=60):
    return pltpu.CompilerParams(
        dimension_semantics=("arbitrary",), vmem_limit_bytes=limit * MIB
    )


def columns(rows, width):
    return pl.BlockSpec((rows, width), lambda i: (0, i))


def fixed(shape):
    return pl.BlockSpec(shape, lambda i: (0,) * len(shape))


def along_tile(count, width):
    return pl.BlockSpec((3, count, width), lambda i: (0, 0, i))


def make_edges(ids, q, k, v, g, taps):
    rows, channels = q.shape
    width = 512
    first = pl.BlockSpec((TAPS, width), lambda i: (0, i))
    last = pl.BlockSpec((TAPS, width), lambda i: (rows // TAPS - 1, i))
    ahead = pl.BlockSpec((EDGE, width), lambda i: ((rows - TAPS) // EDGE - 1, i))
    tail = pl.BlockSpec((EDGE, width), lambda i: (rows // EDGE - 1, i))
    return pl.pallas_call(
        edges_kernel,
        grid=(channels // width,),
        in_specs=[pl.BlockSpec(memory_space=pltpu.SMEM), first, first, ahead, last, ahead, last]
        + [tail, along_tile(SHORT, width)],
        out_specs=[columns(TAPS + 3 * EDGE, width), columns(TAPS + 2 * EDGE, width)],
        out_shape=[
            jax.ShapeDtypeStruct((TAPS + 3 * EDGE, channels), BF16),
            jax.ShapeDtypeStruct((TAPS + 2 * EDGE, channels), BF16),
        ],
        scratch_shapes=[
            pltpu.VMEM((TAPS + EDGE, LANES), F32),
            pltpu.VMEM((TAPS + EDGE, LANES), F32),
            pltpu.VMEM((TAPS, LANES), F32),
            pltpu.VMEM((rows, LANES), F32),
        ],
        compiler_params=params(),
        name="edges",
    )(ids, q, g, k, k, v, v, q, taps)


def make_tables(long_filter):
    groups = long_filter.shape[0]
    wide = pl.BlockSpec((PER_TILE, TAPS, 2 * TAPS), lambda i: (i, 0, 0))
    return pl.pallas_call(
        tables_kernel,
        grid=(groups // PER_TILE,),
        in_specs=[fixed(long_filter.shape)],
        out_specs=[wide, wide],
        out_shape=[jax.ShapeDtypeStruct((groups, TAPS, 2 * TAPS), BF16)] * 2,
        scratch_shapes=[pltpu.VMEM((groups, TAPS), F32)] * 2,
        compiler_params=params(),
        cost_estimate=pl.CostEstimate(
            flops=0, bytes_accessed=32 * groups * TAPS * TAPS, transcendentals=0
        ),
        name="tables",
    )(long_filter)


def make_main(ids, q, k, v, g, taps, skip, fwd, bwd, from_left, from_right):
    rows, channels = q.shape
    tiles = channels // LANES
    wide = pl.BlockSpec((PER_TILE, TAPS, 2 * TAPS), lambda i: (i, 0, 0))
    big = jax.ShapeDtypeStruct((rows, channels), BF16)
    return pl.pallas_call(
        main_kernel,
        grid=(tiles,),
        in_specs=[pl.BlockSpec(memory_space=pltpu.SMEM)]
        + [columns(rows, LANES)] * 4
        + [along_tile(SHORT, LANES), columns(1, LANES), wide, wide]
        + [columns(from_left.shape[0], LANES), columns(from_right.shape[0], LANES)],
        out_specs=[columns(rows, LANES)] * 4
        + [columns(3 * EDGE, LANES), pl.BlockSpec((1, PART_ROWS, LANES), lambda i: (i, 0, 0))],
        out_shape=[big] * 4
        + [
            jax.ShapeDtypeStruct((3 * EDGE, channels), BF16),
            jax.ShapeDtypeStruct((tiles, PART_ROWS, LANES), F32),
        ],
        scratch_shapes=[
            pltpu.VMEM((rows + 2 * EDGE, LANES), F32),
            pltpu.VMEM((rows + EDGE, LANES), F32),
            pltpu.VMEM((rows + EDGE, LANES), F32),
            pltpu.VMEM((rows + TAPS, LANES), BF16),
            pltpu.VMEM((rows + TAPS, LANES), BF16),
            pltpu.VMEM((rows, LANES), F32),
            pltpu.VMEM((rows, LANES), F32),
            pltpu.VMEM((rows, LANES), F32),
            pltpu.VMEM((PER_TILE * TAPS, 2 * TAPS), F32),
            pltpu.VMEM((PER_TILE * TAPS, 2 * TAPS), F32),
            pltpu.VMEM((PER_TILE * TAPS, 2 * TAPS), F32),
            pltpu.VMEM((PER_TILE * 8, LANES), F32),
            pltpu.VMEM((rows, LANES), F32),
        ],
        compiler_params=params(),
        name="main",
    )(ids, q, k, v, g, taps, skip, fwd, bwd, from_left, from_right)


def make_back(which, grads, heads, taps):
    rows, channels = grads.shape
    width = 512
    return pl.pallas_call(
        back_kernel,
        grid=(channels // width,),
        in_specs=[
            columns(rows, width),
            pl.BlockSpec((EDGE, width), lambda i: (which, i)),
            pl.BlockSpec((1, SHORT, width), lambda i: (which, 0, i)),
        ],
        out_specs=columns(rows, width),
        out_shape=jax.ShapeDtypeStruct((rows, channels), BF16),
        scratch_shapes=[pltpu.VMEM((rows + EDGE, LANES), F32)],
        compiler_params=params(),
        cost_estimate=pl.CostEstimate(
            flops=14 * rows * channels, bytes_accessed=8 * rows * channels, transcendentals=0
        ),
        name="back",
    )(grads, heads, taps)


def from_behind(value, steps):
    count = lax.axis_size("seg") * lax.axis_size("ctx")
    first, last = max(0, -steps), min(count, count - steps)
    return lax.ppermute(value, AXES, [(s, s + steps) for s in range(first, last)])


def swap(value, mask):
    count = lax.axis_size("seg") * lax.axis_size("ctx")
    return lax.ppermute(value, AXES, [(s, s ^ mask) for s in range(count)])


def ring_masks(size):
    masks = []
    span = 1
    while span < size:
        masks.append(span if 2 * span < size or size == 2 else span + span // 2)
        span *= 2
    return masks


def total_over_all(value, work):
    ctx = lax.axis_size("ctx")
    seg = lax.axis_size("seg")
    me = lax.axis_index("seg") * ctx + lax.axis_index("ctx")
    cores = 2
    along = 1
    while along * along * cores < seg:
        along *= 2
    halving = [ctx, cores * ctx]
    doubling = [cores * ctx * m for m in ring_masks(along)]
    doubling += [cores * ctx * along * m for m in ring_masks(seg // (cores * along))]
    doubling = [m for m in doubling if m not in halving] + ring_masks(ctx)
    mine = []
    done = []
    pending = list(work)
    for mask in halving:
        half = value.shape[0] // 2
        high = ((me // mask) % 2) == 1
        if mask != ctx:
            high = high ^ (((me // (2 * mask)) % 2) == 1)
        low_part, high_part = value[:half], value[half:]
        mine.append(high)
        got = swap(jnp.where(high, low_part, high_part), mask)
        value = jnp.where(high, high_part, low_part) + got
    for n, mask in enumerate(doubling):
        job = pending.pop(0) if pending and n >= 1 else None
        if job is None:
            value = value + swap(value, mask)
            continue
        run, inputs = job
        value, inputs = lax.optimization_barrier((value, inputs))
        got = swap(value, mask)
        value, result = lax.optimization_barrier((value + got, run(*inputs)))
        done.append(result)
    done += [run(*inputs) for run, inputs in pending]
    for mask, high in zip(reversed(halving), reversed(mine)):
        got = swap(value, mask)
        value = jnp.where(
            high, jnp.concatenate([got, value]), jnp.concatenate([value, got])
        )
    return value, done


def per_device(
    token_ids, query_in, key_in, value_in, short_filters, long_filter, skip_gain, out_grad
):
    length, channels = query_in.shape
    tiles = channels // LANES
    to_right, to_left = make_edges(
        token_ids, query_in, key_in, value_in, out_grad, short_filters
    )
    from_left = from_behind(to_right, 1)
    from_right = from_behind(to_left, -1)
    fwd, bwd = make_tables(long_filter)
    out, gq, gk, gv, heads, part = make_main(
        token_ids, query_in, key_in, value_in, out_grad, short_filters,
        skip_gain.reshape(1, channels), fwd, bwd, from_left, from_right,
    )
    next_heads = from_behind(heads, -1)
    jobs = [
        (functools.partial(make_back, i), (grads, next_heads, short_filters))
        for i, grads in enumerate((gq, gk, gv))
    ]
    total, (grad_query, grad_key, grad_value) = total_over_all(
        part.reshape(tiles * PART_ROWS, LANES), jobs
    )
    norm_scale = float(length * lax.axis_size("seg") * lax.axis_size("ctx")) ** (-0.5)
    total = total.reshape(tiles, PART_ROWS, LANES) * norm_scale
    grad_long = total[:, :PER_TILE].reshape(tiles * PER_TILE, TAPS)
    short_lines = 3 * SHORT
    grad_short = (
        total[:, PER_TILE : PER_TILE + short_lines]
        .transpose(1, 0, 2)
        .reshape(3, SHORT, channels)
    )
    grad_skip = total[:, PER_TILE + short_lines].reshape(channels)
    return out, grad_query, grad_key, grad_value, grad_long, grad_skip, grad_short


def solution(mesh):
    sharded = P(("seg", "ctx"), None)
    return jax.shard_map(
        per_device,
        mesh=mesh,
        in_specs=(P(("seg", "ctx")), sharded, sharded, sharded, P(), P(), P(), sharded),
        out_specs=(sharded, sharded, sharded, sharded, P(), P(), P()),
        check_vma=False,
    )
```

```python
import functools

import jax
import jax.numpy as jnp
from jax import lax
from jax.experimental import pallas as pl
from jax.experimental.pallas import tpu as pltpu
from jax.sharding import PartitionSpec as P

GROUP = 16
TAPS = 128
SHORT = 7
LANES = 128
PER_TILE = LANES // GROUP
EDGE = 16
RUN = 32
PART_ROWS = 32
PER_STEP = 2
WIDE = PER_STEP * LANES
STEP = 64
TAIL = 8
AXES = ("seg", "ctx")
MIB = 1024 * 1024
F32 = jnp.float32
BF16 = jnp.bfloat16


def causal(frame, which, taps, start, count):
    total = taps[which, 0:1] * frame[pl.ds(start, count)]
    for j in range(1, SHORT):
        total = total + taps[which, j : j + 1] * frame[pl.ds(start - j, count)]
    return total


def weight_of(repeat):
    return jnp.where(repeat > 0.5, F32(0.1), F32(1.0))


def mark_repeats(ids, marks):
    rows = marks.shape[0]
    row = lax.broadcasted_iota(jnp.int32, (RUN, LANES), 0)

    def mark(at):
        return jnp.full((RUN, LANES), (ids[at] >= 97).astype(F32))

    for r in range(0, rows, RUN):
        run = mark(r + 1)
        if r == 0:
            run = jnp.where(row == 0, mark(0), run)
        if r + RUN == rows:
            run = jnp.where(row == RUN - 1, mark(rows - 1), run)
        marks[r : r + RUN] = run


def edges_kernel(
    ids, q, g, k_edge, k, v_edge, v, q_tail, taps_ref, right, left, kf, vf, qf, rep
):
    @pl.when(pl.program_id(0) == 0)
    def _():
        mark_repeats(ids, rep)

    for lt in range(q.shape[1] // LANES):
        ls = slice(lt * LANES, (lt + 1) * LANES)
        taps = taps_ref[:, :, ls]
        kf[:EDGE] = k_edge[:, ls].astype(F32)
        vf[:EDGE] = v_edge[:, ls].astype(F32)
        kf[EDGE:] = k[:, ls].astype(F32)
        vf[EDGE:] = v[:, ls].astype(F32)
        qf[...] = q[:, ls].astype(F32)
        for r in range(0, TAPS, 64):
            act_k = causal(kf, 1, taps, EDGE + r, 64)
            act_v = causal(vf, 2, taps, EDGE + r, 64)
            right[r : r + 64, ls] = (act_k * act_v).astype(BF16)
        tails = [kf[TAPS + EDGE - TAIL :], vf[TAPS + EDGE - TAIL :]]
        tails += [q_tail[:, ls].astype(F32)[EDGE - TAIL :], jnp.zeros((TAIL, LANES), F32)]
        right[TAPS:, ls] = jnp.concatenate(tails, axis=0).astype(BF16)
        for r, count in ((EDGE, 48), (EDGE + 48, 64)):
            act_q = causal(qf, 0, taps, r, count)
            grad = g[r : r + count, ls].astype(F32) * weight_of(rep[r : r + count])
            left[r - EDGE : r - EDGE + count, ls] = (grad * act_q).astype(BF16)
        left[TAPS - EDGE : TAPS, ls] = q[:EDGE, ls]
        left[TAPS : TAPS + EDGE, ls] = g[:EDGE, ls]
        left[TAPS + EDGE : TAPS + 2 * EDGE, ls] = rep[:EDGE].astype(BF16)


def tables_kernel(taps, fwd, bwd, plain, backwards):
    row = lax.broadcasted_iota(jnp.int32, (TAPS, TAPS), 0)
    col = lax.broadcasted_iota(jnp.int32, (TAPS, TAPS), 1)
    tile = pl.program_id(0)

    @pl.when(tile == 0)
    def _():
        mirror = ((row + col == TAPS) | ((row == 0) & (col == 0))).astype(BF16)
        plain[...] = taps[...].astype(F32)
        backwards[...] = jnp.dot(taps[...], mirror, preferred_element_type=F32)

    first = pl.multiple_of(tile * PER_TILE, PER_TILE)
    plain_rows = plain[pl.ds(first, PER_TILE)]
    backward_rows = backwards[pl.ds(first, PER_TILE)]

    def rings(source, g):
        spread = jnp.broadcast_to(source[g : g + 1], (TAPS, TAPS))
        return pltpu.roll(spread, 0, 1, stride=1, stride_axis=0)

    for g in range(PER_TILE):
        ring = rings(backward_rows, g)
        fwd[g, :, :TAPS] = jnp.where(col > row, ring, 0.0).astype(BF16)
        fwd[g, :, TAPS:] = jnp.where(col <= row, ring, 0.0).astype(BF16)
        ring = rings(plain_rows, g)
        bwd[g, :, :TAPS] = jnp.where(col >= row, ring, 0.0).astype(BF16)
        bwd[g, :, TAPS:] = jnp.where(col < row, ring, 0.0).astype(BF16)


def together(*jobs):
    jobs = list(jobs)
    while jobs:
        for job in list(jobs):
            if next(job, jobs) is jobs:
                jobs.remove(job)


def short_sums(sums, grads, frame, start):
    wide = grads.astype(F32)
    count = wide.shape[0]
    for j in range(SHORT):
        both = wide * frame[pl.ds(start - j, count)]
        sums[j] = sums[j] + jnp.sum(both.reshape(count // 8, 8, LANES), axis=0)


def own_groups(prod, r, count):
    block, at = divmod(r, TAPS)
    ls = slice(block * LANES, (block + 1) * LANES)
    lane = lax.broadcasted_iota(jnp.int32, (count, LANES), 1) // GROUP
    total = prod[at : at + count, ls]
    for n in range(1, PER_TILE):
        total = jnp.where(lane == n, prod[n * TAPS + at : n * TAPS + at + count, ls], total)
    return total


class Tile:
    def __init__(self, refs, taps, skip, rep, scratch):
        (self.q, self.k, self.v, self.g, self.fwd, self.bwd, self.from_left, self.from_right,
         self.out, self.gq, self.gk, self.gv, self.heads, self.part) = refs
        (self.qf, self.kf, self.vf, self.xs, self.gs, self.act_q, self.act_k, self.act_v,
         self.prod_p, self.prod_f, self.prod_b, self.diag) = scratch
        self.taps, self.skip, self.rep = taps, skip, rep
        self.rows = self.q.shape[0]
        self.sums = [[jnp.zeros((8, LANES), F32)] * SHORT for _ in range(3)]
        self.skip_sum = jnp.zeros((8, LANES), F32)

    def activations(self):
        rows, taps, qf, kf, vf = self.rows, self.taps, self.qf, self.kf, self.vf
        from_left, from_right = self.from_left, self.from_right
        qf[EDGE : EDGE + rows] = self.q[...].astype(F32)
        kf[EDGE : EDGE + rows] = self.k[...].astype(F32)
        vf[EDGE : EDGE + rows] = self.v[...].astype(F32)
        tails = from_left[TAPS:].astype(F32)
        kf[EDGE - TAIL : EDGE] = tails[:TAIL]
        vf[EDGE - TAIL : EDGE] = tails[TAIL : 2 * TAIL]
        qf[EDGE - TAIL : EDGE] = tails[2 * TAIL : 3 * TAIL]
        qf[EDGE + rows :] = from_right[TAPS - EDGE : TAPS].astype(F32)
        self.xs[:TAPS] = from_left[:TAPS]
        self.gs[rows + EDGE :] = from_right[: TAPS - EDGE]
        grad = from_right[TAPS : TAPS + EDGE].astype(F32) * weight_of(
            from_right[TAPS + EDGE : TAPS + 2 * EDGE].astype(F32)
        )
        a_q = causal(qf, 0, taps, EDGE + rows, EDGE)
        self.gs[rows : rows + EDGE] = (grad * a_q).astype(BF16)
        for r in range(0, rows, STEP):
            a_q = causal(qf, 0, taps, EDGE + r, STEP)
            a_k = causal(kf, 1, taps, EDGE + r, STEP)
            a_v = causal(vf, 2, taps, EDGE + r, STEP)
            self.act_q[r : r + STEP] = a_q
            self.act_k[r : r + STEP] = a_k
            self.act_v[r : r + STEP] = a_v
            gated = (a_k * a_v).astype(BF16)
            self.xs[TAPS + r : TAPS + r + STEP] = gated
            grad = self.g[r : r + STEP].astype(F32) * weight_of(self.rep[r : r + STEP])
            scaled = (grad * a_q).astype(BF16)
            self.gs[r : r + STEP] = scaled
            both = scaled.astype(F32) * gated.astype(F32)
            self.skip_sum = self.skip_sum + jnp.sum(both.reshape(STEP // 8, 8, LANES), axis=0)
            yield

    def window(self, rows_of):
        return jnp.concatenate([rows_of[: 2 * TAPS], rows_of[TAPS:]], axis=1)

    def filter_products(self, table, rows_of, prod):
        whole = table[...].reshape(PER_TILE * TAPS, 2 * TAPS)
        prod[...] = jnp.dot(whole, self.window(rows_of), preferred_element_type=F32)
        yield

    def forward_products(self):
        return self.filter_products(self.fwd, self.xs, self.prod_f)

    def backward_products(self):
        return self.filter_products(self.bwd, self.gs, self.prod_b)

    def pair_products(self):
        windows = self.window(self.gs)
        own_x = jnp.concatenate([self.xs[TAPS : 2 * TAPS], self.xs[2 * TAPS :]], axis=1)
        lane = lax.broadcasted_iota(jnp.int32, own_x.shape, 1) % LANES // GROUP
        masked = jnp.concatenate(
            [jnp.where(lane == n, own_x, jnp.zeros_like(own_x)) for n in range(PER_TILE)],
            axis=0,
        )
        self.prod_p[...] = lax.dot_general(
            masked, windows, (((1,), (1,)), ((), ())), preferred_element_type=F32
        )
        yield

    def query_side(self):
        for r in range(0, self.rows, STEP):
            gated = self.xs[TAPS + r : TAPS + r + STEP].astype(F32)
            filtered = own_groups(self.prod_f, r, STEP) + self.skip * gated
            self.out[r : r + STEP] = (self.act_q[r : r + STEP] * filtered).astype(BF16)
            grad = self.g[r : r + STEP].astype(F32) * weight_of(self.rep[r : r + STEP])
            grads = (grad * filtered).astype(BF16)
            self.gq[r : r + STEP] = grads
            short_sums(self.sums[0], grads, self.qf, EDGE + r)
            yield

    def key_value_side(self):
        for r in range(0, self.rows, STEP):
            scaled = self.gs[r : r + STEP].astype(F32)
            grad_gated = self.skip * scaled + own_groups(self.prod_b, r, STEP)
            grads = (grad_gated * self.act_v[r : r + STEP]).astype(BF16)
            self.gk[r : r + STEP] = grads
            short_sums(self.sums[1], grads, self.kf, EDGE + r)
            grads = (grad_gated * self.act_k[r : r + STEP]).astype(BF16)
            self.gv[r : r + STEP] = grads
            short_sums(self.sums[2], grads, self.vf, EDGE + r)
            yield

    def diagonals(self):
        sub = lax.broadcasted_iota(jnp.int32, (8, LANES), 0)
        lane = lax.broadcasted_iota(jnp.int32, (8, LANES), 1)
        prod = self.prod_p
        for n in range(PER_TILE):
            total = jnp.zeros((8, LANES), F32)
            for m in range(TAPS // 8):
                r = n * TAPS + m * 8
                ring = jnp.where(
                    lane >= sub + m * 8, prod[r : r + 8, :LANES], prod[r : r + 8, LANES:]
                )
                total = total + (pltpu.roll(ring, LANES - 8 * m, 1) if m else ring)
            self.diag[n * 8 : n * 8 + 8] = total
            if n % 2:
                yield
        lines = self.diag[pl.ds(0, PER_TILE, stride=8)]
        for r in range(1, 8):
            row = self.diag[pl.ds(r, PER_TILE, stride=8)]
            lines = lines + pltpu.roll(row, LANES - r, 1)
        self.part[:PER_TILE] = lines

    def finish(self):
        self.heads[:EDGE] = self.gq[:EDGE]
        self.heads[EDGE : 2 * EDGE] = self.gk[:EDGE]
        self.heads[2 * EDGE :] = self.gv[:EDGE]
        every = self.sums[0] + self.sums[1] + self.sums[2] + [self.skip_sum]
        lines = [jnp.sum(one, axis=0, keepdims=True) for one in every]
        lines.append(jnp.zeros((PART_ROWS - PER_TILE - len(lines), LANES), F32))
        self.part[PER_TILE:] = jnp.concatenate(lines, axis=0)
        yield


def main_kernel(
    ids, q, k, v, g, taps_ref, skip_ref, fwd, bwd, from_left, from_right,
    out, gq, gk, gv, heads, part, rep, *scratch,
):
    @pl.when(pl.program_id(0) == 0)
    def _():
        mark_repeats(ids, rep)

    each = len(scratch) // PER_STEP
    tiles = []
    for lt in range(PER_STEP):
        ls = slice(lt * LANES, (lt + 1) * LANES)
        tables = slice(lt * PER_TILE, (lt + 1) * PER_TILE)
        refs = [ref.at[:, ls] for ref in (q, k, v, g)]
        refs += [fwd.at[tables], bwd.at[tables]]
        refs += [ref.at[:, ls] for ref in (from_left, from_right, out, gq, gk, gv, heads)]
        refs += [part.at[lt]]
        own = scratch[lt * each : (lt + 1) * each]
        tiles.append(Tile(refs, taps_ref[:, :, ls], skip_ref[:, ls], rep, own))
    together(tiles[0].activations())
    for n, tile in enumerate(tiles):
        following = tiles[n + 1 : n + 2]
        if n == 0:
            together(tile.forward_products(), *[t.activations() for t in following])
        together(tile.backward_products(), tile.query_side())
        together(tile.pair_products(), tile.key_value_side())
        together(
            tile.diagonals(), *[t.forward_products() for t in following], tile.finish()
        )


def back_kernel(grads, heads, taps_ref, result, frame):
    rows = grads.shape[0]
    step = 64
    for lt in range(grads.shape[1] // LANES):
        ls = slice(lt * LANES, (lt + 1) * LANES)
        frame[:rows] = grads[:, ls].astype(F32)
        frame[rows:] = heads[:, ls].astype(F32)
        for r in range(0, rows, step):
            total = taps_ref[0, 0:1, ls] * frame[pl.ds(r, step)]
            for j in range(1, SHORT):
                total = total + taps_ref[0, j : j + 1, ls] * frame[pl.ds(r + j, step)]
            result[r : r + step, ls] = total.astype(BF16)


def params(limit=60):
    return pltpu.CompilerParams(
        dimension_semantics=("arbitrary",), vmem_limit_bytes=limit * MIB
    )


def columns(rows, width):
    return pl.BlockSpec((rows, width), lambda i: (0, i))


def fixed(shape):
    return pl.BlockSpec(shape, lambda i: (0,) * len(shape))


def along_tile(count, width):
    return pl.BlockSpec((3, count, width), lambda i: (0, 0, i))


def make_edges(ids, q, k, v, g, taps):
    rows, channels = q.shape
    width = 1024
    first = pl.BlockSpec((TAPS, width), lambda i: (0, i))
    last = pl.BlockSpec((TAPS, width), lambda i: (rows // TAPS - 1, i))
    ahead = pl.BlockSpec((EDGE, width), lambda i: ((rows - TAPS) // EDGE - 1, i))
    tail = pl.BlockSpec((EDGE, width), lambda i: (rows // EDGE - 1, i))
    return pl.pallas_call(
        edges_kernel,
        grid=(channels // width,),
        in_specs=[pl.BlockSpec(memory_space=pltpu.SMEM), first, first, ahead, last, ahead, last]
        + [tail, along_tile(SHORT, width)],
        out_specs=[columns(TAPS + 2 * EDGE, width), columns(TAPS + 2 * EDGE, width)],
        out_shape=[
            jax.ShapeDtypeStruct((TAPS + 2 * EDGE, channels), BF16),
            jax.ShapeDtypeStruct((TAPS + 2 * EDGE, channels), BF16),
        ],
        scratch_shapes=[
            pltpu.VMEM((TAPS + EDGE, LANES), F32),
            pltpu.VMEM((TAPS + EDGE, LANES), F32),
            pltpu.VMEM((TAPS, LANES), F32),
            pltpu.VMEM((rows, LANES), F32),
        ],
        compiler_params=params(),
        name="edges",
    )(ids, q, g, k, k, v, v, q, taps)


def make_tables(long_filter):
    groups = long_filter.shape[0]
    wide = pl.BlockSpec((PER_TILE, TAPS, 2 * TAPS), lambda i: (i, 0, 0))
    return pl.pallas_call(
        tables_kernel,
        grid=(groups // PER_TILE,),
        in_specs=[fixed(long_filter.shape)],
        out_specs=[wide, wide],
        out_shape=[jax.ShapeDtypeStruct((groups, TAPS, 2 * TAPS), BF16)] * 2,
        scratch_shapes=[pltpu.VMEM((groups, TAPS), F32)] * 2,
        compiler_params=params(),
        cost_estimate=pl.CostEstimate(
            flops=0, bytes_accessed=32 * groups * TAPS * TAPS, transcendentals=0
        ),
        name="tables",
    )(long_filter)


def make_main(ids, q, k, v, g, taps, skip, fwd, bwd, from_left, from_right):
    rows, channels = q.shape
    tiles = channels // LANES
    wide = pl.BlockSpec((PER_STEP * PER_TILE, TAPS, 2 * TAPS), lambda i: (i, 0, 0))
    big = jax.ShapeDtypeStruct((rows, channels), BF16)
    return pl.pallas_call(
        main_kernel,
        grid=(tiles // PER_STEP,),
        in_specs=[pl.BlockSpec(memory_space=pltpu.SMEM)]
        + [columns(rows, WIDE)] * 4
        + [along_tile(SHORT, WIDE), columns(1, WIDE), wide, wide]
        + [columns(from_left.shape[0], WIDE), columns(from_right.shape[0], WIDE)],
        out_specs=[columns(rows, WIDE)] * 4
        + [columns(3 * EDGE, WIDE), pl.BlockSpec((PER_STEP, PART_ROWS, LANES), lambda i: (i, 0, 0))],
        out_shape=[big] * 4
        + [
            jax.ShapeDtypeStruct((3 * EDGE, channels), BF16),
            jax.ShapeDtypeStruct((tiles, PART_ROWS, LANES), F32),
        ],
        scratch_shapes=[pltpu.VMEM((rows, LANES), F32)]
        + PER_STEP
        * [
            pltpu.VMEM((rows + 2 * EDGE, LANES), F32),
            pltpu.VMEM((rows + EDGE, LANES), F32),
            pltpu.VMEM((rows + EDGE, LANES), F32),
            pltpu.VMEM((rows + TAPS, LANES), BF16),
            pltpu.VMEM((rows + TAPS, LANES), BF16),
            pltpu.VMEM((rows, LANES), F32),
            pltpu.VMEM((rows, LANES), F32),
            pltpu.VMEM((rows, LANES), F32),
            pltpu.VMEM((PER_TILE * TAPS, 2 * TAPS), F32),
            pltpu.VMEM((PER_TILE * TAPS, 2 * TAPS), F32),
            pltpu.VMEM((PER_TILE * TAPS, 2 * TAPS), F32),
            pltpu.VMEM((PER_TILE * 8, LANES), F32),
        ],
        compiler_params=params(),
        name="main",
    )(ids, q, k, v, g, taps, skip, fwd, bwd, from_left, from_right)


def make_back(which, grads, heads, taps):
    rows, channels = grads.shape
    width = 1024
    return pl.pallas_call(
        back_kernel,
        grid=(channels // width,),
        in_specs=[
            columns(rows, width),
            pl.BlockSpec((EDGE, width), lambda i: (which, i)),
            pl.BlockSpec((1, SHORT, width), lambda i: (which, 0, i)),
        ],
        out_specs=columns(rows, width),
        out_shape=jax.ShapeDtypeStruct((rows, channels), BF16),
        scratch_shapes=[pltpu.VMEM((rows + EDGE, LANES), F32)],
        compiler_params=params(),
        cost_estimate=pl.CostEstimate(
            flops=14 * rows * channels, bytes_accessed=8 * rows * channels, transcendentals=0
        ),
        name="back",
    )(grads, heads, taps)


def last_kernel(scale, which, half, other, long_grad, skip_grad, short_grad):
    mine = which[0]
    tiles = 2 * half.shape[0] // PART_ROWS
    for tile in range(tiles):
        side, at = divmod(tile, tiles // 2)
        rows = slice(at * PART_ROWS, (at + 1) * PART_ROWS)
        both = jnp.where(mine == side, half[rows], other[rows]) * scale
        ls = slice(tile * LANES, (tile + 1) * LANES)
        long_grad[tile * PER_TILE : (tile + 1) * PER_TILE] = both[:PER_TILE]
        for i in range(3):
            first = PER_TILE + i * SHORT
            short_grad[i, :, ls] = both[first : first + SHORT]
        skip_grad[ls] = both[PER_TILE + 3 * SHORT]


def make_last(half, other, which, scale):
    tiles = 2 * half.shape[0] // PART_ROWS
    channels = tiles * LANES
    return pl.pallas_call(
        functools.partial(last_kernel, scale),
        in_specs=[pl.BlockSpec(memory_space=pltpu.SMEM)]
        + [pl.BlockSpec(memory_space=pltpu.VMEM)] * 2,
        out_specs=[pl.BlockSpec(memory_space=pltpu.VMEM)] * 3,
        out_shape=[
            jax.ShapeDtypeStruct((tiles * PER_TILE, TAPS), F32),
            jax.ShapeDtypeStruct((channels,), F32),
            jax.ShapeDtypeStruct((3, SHORT, channels), F32),
        ],
        compiler_params=pltpu.CompilerParams(vmem_limit_bytes=4 * MIB),
        name="last",
    )(which.reshape(1).astype(jnp.int32), half, other)


def from_behind(value, steps):
    count = lax.axis_size("seg") * lax.axis_size("ctx")
    first, last = max(0, -steps), min(count, count - steps)
    return lax.ppermute(value, AXES, [(s, s + steps) for s in range(first, last)])


def swap(value, mask):
    count = lax.axis_size("seg") * lax.axis_size("ctx")
    return lax.ppermute(value, AXES, [(s, s ^ mask) for s in range(count)])


def ring_masks(size):
    masks = []
    span = 1
    while span < size:
        masks.append(span if 2 * span < size or size == 2 else span + span // 2)
        span *= 2
    return masks


def total_over_all(value, work):
    ctx = lax.axis_size("ctx")
    seg = lax.axis_size("seg")
    me = lax.axis_index("seg") * ctx + lax.axis_index("ctx")
    cores = 2
    along = 1
    while along * along * cores < seg:
        along *= 2
    halving = [ctx, cores * ctx]
    doubling = [cores * ctx * m for m in ring_masks(along)]
    doubling += [cores * ctx * along * m for m in ring_masks(seg // (cores * along))]
    doubling = [m for m in doubling if m not in halving] + ring_masks(ctx)
    mine = []
    done = []
    pending = list(work)
    for mask in halving:
        half = value.shape[0] // 2
        high = ((me // mask) % 2) == 1
        if mask != ctx:
            high = high ^ (((me // (2 * mask)) % 2) == 1)
        low_part, high_part = value[:half], value[half:]
        mine.append(high)
        got = swap(jnp.where(high, low_part, high_part), mask)
        value = jnp.where(high, high_part, low_part) + got
    for n, mask in enumerate(doubling):
        job = pending.pop(0) if pending and n >= 1 else None
        if job is None:
            value = value + swap(value, mask)
            continue
        run, inputs = job
        value, inputs = lax.optimization_barrier((value, inputs))
        got = swap(value, mask)
        value, result = lax.optimization_barrier((value + got, run(*inputs)))
        done.append(result)
    done += [run(*inputs) for run, inputs in pending]
    for mask, high in zip(halving[:0:-1], mine[:0:-1]):
        got = swap(value, mask)
        value = jnp.where(
            high, jnp.concatenate([got, value]), jnp.concatenate([value, got])
        )
    return value, swap(value, halving[0]), mine[0], done


def per_device(
    token_ids, query_in, key_in, value_in, short_filters, long_filter, skip_gain, out_grad
):
    length, channels = query_in.shape
    tiles = channels // LANES
    to_right, to_left = make_edges(
        token_ids, query_in, key_in, value_in, out_grad, short_filters
    )
    from_left = from_behind(to_right, 1)
    from_right = from_behind(to_left, -1)
    fwd, bwd = make_tables(long_filter)
    out, gq, gk, gv, heads, part = make_main(
        token_ids, query_in, key_in, value_in, out_grad, short_filters,
        skip_gain.reshape(1, channels), fwd, bwd, from_left, from_right,
    )
    next_heads = from_behind(heads, -1)
    jobs = [
        (functools.partial(make_back, i), (grads, next_heads, short_filters))
        for i, grads in enumerate((gq, gk, gv))
    ]
    half, other, which, (grad_query, grad_key, grad_value) = total_over_all(
        part.reshape(tiles * PART_ROWS, LANES), jobs
    )
    norm_scale = float(length * lax.axis_size("seg") * lax.axis_size("ctx")) ** (-0.5)
    grad_long, grad_skip, grad_short = make_last(half, other, which, norm_scale)
    return out, grad_query, grad_key, grad_value, grad_long, grad_skip, grad_short


def solution(mesh):
    sharded = P(("seg", "ctx"), None)
    return jax.shard_map(
        per_device,
        mesh=mesh,
        in_specs=(P(("seg", "ctx")), sharded, sharded, sharded, P(), P(), P(), sharded),
        out_specs=(sharded, sharded, sharded, sharded, P(), P(), P()),
        check_vma=False,
    )
```

```python
import functools

import jax
import jax.numpy as jnp
from jax import lax
from jax.experimental import pallas as pl
from jax.experimental.pallas import tpu as pltpu
from jax.sharding import PartitionSpec as P

GROUP = 16
TAPS = 128
SHORT = 7
LANES = 128
PER_TILE = LANES // GROUP
EDGE = 16
RUN = 32
PART_ROWS = 32
PER_STEP = 2
WIDE = PER_STEP * LANES
STEP = 64
TAIL = 8
AXES = ("seg", "ctx")
MIB = 1024 * 1024
F32 = jnp.float32
BF16 = jnp.bfloat16


def causal(frame, which, taps, start, count):
    total = taps[which, 0:1] * frame[pl.ds(start, count)]
    for j in range(1, SHORT):
        total = total + taps[which, j : j + 1] * frame[pl.ds(start - j, count)]
    return total


def weight_of(repeat):
    return jnp.where(repeat > 0.5, F32(0.1), F32(1.0))


def mark_repeats(ids, marks):
    rows = marks.shape[0]
    row = lax.broadcasted_iota(jnp.int32, (RUN, LANES), 0)

    def mark(at):
        return jnp.full((RUN, LANES), (ids[at] >= 97).astype(F32))

    for r in range(0, rows, RUN):
        run = mark(r + 1)
        if r == 0:
            run = jnp.where(row == 0, mark(0), run)
        if r + RUN == rows:
            run = jnp.where(row == RUN - 1, mark(rows - 1), run)
        marks[r : r + RUN] = run


def edges_kernel(
    ids, q, g, k_edge, k, v_edge, v, q_tail, taps_ref, right, left, kf, vf, qf, rep
):
    @pl.when(pl.program_id(0) == 0)
    def _():
        mark_repeats(ids, rep)

    for lt in range(q.shape[1] // LANES):
        ls = slice(lt * LANES, (lt + 1) * LANES)
        taps = taps_ref[:, :, ls]
        kf[:EDGE] = k_edge[:, ls].astype(F32)
        vf[:EDGE] = v_edge[:, ls].astype(F32)
        kf[EDGE:] = k[:, ls].astype(F32)
        vf[EDGE:] = v[:, ls].astype(F32)
        qf[...] = q[:, ls].astype(F32)
        for r in range(0, TAPS, 64):
            act_k = causal(kf, 1, taps, EDGE + r, 64)
            act_v = causal(vf, 2, taps, EDGE + r, 64)
            right[r : r + 64, ls] = (act_k * act_v).astype(BF16)
        tails = [kf[TAPS + EDGE - TAIL :], vf[TAPS + EDGE - TAIL :]]
        tails += [q_tail[:, ls].astype(F32)[EDGE - TAIL :], jnp.zeros((TAIL, LANES), F32)]
        right[TAPS:, ls] = jnp.concatenate(tails, axis=0).astype(BF16)
        for r, count in ((EDGE, 48), (EDGE + 48, 64)):
            act_q = causal(qf, 0, taps, r, count)
            grad = g[r : r + count, ls].astype(F32) * weight_of(rep[r : r + count])
            left[r - EDGE : r - EDGE + count, ls] = (grad * act_q).astype(BF16)
        left[TAPS - EDGE : TAPS, ls] = q[:EDGE, ls]
        left[TAPS : TAPS + EDGE, ls] = g[:EDGE, ls]
        left[TAPS + EDGE : TAPS + 2 * EDGE, ls] = rep[:EDGE].astype(BF16)


def tables_kernel(taps, fwd, bwd, plain, backwards):
    row = lax.broadcasted_iota(jnp.int32, (TAPS, TAPS), 0)
    col = lax.broadcasted_iota(jnp.int32, (TAPS, TAPS), 1)
    tile = pl.program_id(0)

    @pl.when(tile == 0)
    def _():
        mirror = ((row + col == TAPS) | ((row == 0) & (col == 0))).astype(BF16)
        plain[...] = taps[...].astype(F32)
        backwards[...] = jnp.dot(taps[...], mirror, preferred_element_type=F32)

    first = pl.multiple_of(tile * PER_TILE, PER_TILE)
    plain_rows = plain[pl.ds(first, PER_TILE)]
    backward_rows = backwards[pl.ds(first, PER_TILE)]

    def rings(source, g):
        spread = jnp.broadcast_to(source[g : g + 1], (TAPS, TAPS))
        return pltpu.roll(spread, 0, 1, stride=1, stride_axis=0)

    for g in range(PER_TILE):
        ring = rings(backward_rows, g)
        fwd[g, :, :TAPS] = jnp.where(col > row, ring, 0.0).astype(BF16)
        fwd[g, :, TAPS:] = jnp.where(col <= row, ring, 0.0).astype(BF16)
        ring = rings(plain_rows, g)
        bwd[g, :, :TAPS] = jnp.where(col >= row, ring, 0.0).astype(BF16)
        bwd[g, :, TAPS:] = jnp.where(col < row, ring, 0.0).astype(BF16)


def together(*jobs):
    jobs = list(jobs)
    while jobs:
        for job in list(jobs):
            if next(job, jobs) is jobs:
                jobs.remove(job)


def short_sums(sums, grads, frame, start):
    wide = grads.astype(F32)
    count = wide.shape[0]
    for j in range(SHORT):
        both = wide * frame[pl.ds(start - j, count)]
        sums[j] = sums[j] + jnp.sum(both.reshape(count // 8, 8, LANES), axis=0)


def own_groups(prod, r, count):
    block, at = divmod(r, TAPS)
    ls = slice(block * LANES, (block + 1) * LANES)
    lane = lax.broadcasted_iota(jnp.int32, (count, LANES), 1) // GROUP
    total = prod[at : at + count, ls]
    for n in range(1, PER_TILE):
        total = jnp.where(lane == n, prod[n * TAPS + at : n * TAPS + at + count, ls], total)
    return total


class Tile:
    def __init__(self, refs, taps, skip, rep, scratch):
        (self.q, self.k, self.v, self.g, self.fwd, self.bwd, self.from_left, self.from_right,
         self.out, self.gq, self.gk, self.gv, self.heads, self.part) = refs
        (self.qf, self.kf, self.vf, self.xs, self.gs, self.act_q, self.act_k, self.act_v,
         self.prod_p, self.prod_f, self.prod_b, self.diag) = scratch
        self.taps, self.skip, self.rep = taps, skip, rep
        self.rows = self.q.shape[0]
        self.sums = [[jnp.zeros((8, LANES), F32)] * SHORT for _ in range(3)]
        self.skip_sum = jnp.zeros((8, LANES), F32)

    def activations(self):
        rows, taps, qf, kf, vf = self.rows, self.taps, self.qf, self.kf, self.vf
        from_left, from_right = self.from_left, self.from_right
        qf[EDGE : EDGE + rows] = self.q[...].astype(F32)
        kf[EDGE : EDGE + rows] = self.k[...].astype(F32)
        vf[EDGE : EDGE + rows] = self.v[...].astype(F32)
        tails = from_left[TAPS:].astype(F32)
        kf[EDGE - TAIL : EDGE] = tails[:TAIL]
        vf[EDGE - TAIL : EDGE] = tails[TAIL : 2 * TAIL]
        qf[EDGE - TAIL : EDGE] = tails[2 * TAIL : 3 * TAIL]
        qf[EDGE + rows :] = from_right[TAPS - EDGE : TAPS].astype(F32)
        self.xs[:TAPS] = from_left[:TAPS]
        self.gs[rows + EDGE :] = from_right[: TAPS - EDGE]
        grad = from_right[TAPS : TAPS + EDGE].astype(F32) * weight_of(
            from_right[TAPS + EDGE : TAPS + 2 * EDGE].astype(F32)
        )
        a_q = causal(qf, 0, taps, EDGE + rows, EDGE)
        self.gs[rows : rows + EDGE] = (grad * a_q).astype(BF16)
        for r in range(0, rows, STEP):
            a_q = causal(qf, 0, taps, EDGE + r, STEP)
            a_k = causal(kf, 1, taps, EDGE + r, STEP)
            a_v = causal(vf, 2, taps, EDGE + r, STEP)
            self.act_q[r : r + STEP] = a_q
            self.act_k[r : r + STEP] = a_k
            self.act_v[r : r + STEP] = a_v
            gated = (a_k * a_v).astype(BF16)
            self.xs[TAPS + r : TAPS + r + STEP] = gated
            grad = self.g[r : r + STEP].astype(F32) * weight_of(self.rep[r : r + STEP])
            scaled = (grad * a_q).astype(BF16)
            self.gs[r : r + STEP] = scaled
            both = scaled.astype(F32) * gated.astype(F32)
            self.skip_sum = self.skip_sum + jnp.sum(both.reshape(STEP // 8, 8, LANES), axis=0)
            yield

    def window(self, rows_of):
        return jnp.concatenate([rows_of[: 2 * TAPS], rows_of[TAPS:]], axis=1)

    def filter_products(self, table, rows_of, prod):
        whole = table[...].reshape(PER_TILE * TAPS, 2 * TAPS)
        prod[...] = jnp.dot(whole, self.window(rows_of), preferred_element_type=F32)
        yield

    def forward_products(self):
        return self.filter_products(self.fwd, self.xs, self.prod_f)

    def backward_products(self):
        return self.filter_products(self.bwd, self.gs, self.prod_b)

    def pair_products(self):
        windows = self.window(self.gs)
        own_x = jnp.concatenate([self.xs[TAPS : 2 * TAPS], self.xs[2 * TAPS :]], axis=1)
        lane = lax.broadcasted_iota(jnp.int32, own_x.shape, 1) % LANES // GROUP
        masked = jnp.concatenate(
            [jnp.where(lane == n, own_x, jnp.zeros_like(own_x)) for n in range(PER_TILE)],
            axis=0,
        )
        self.prod_p[...] = lax.dot_general(
            masked, windows, (((1,), (1,)), ((), ())), preferred_element_type=F32
        )
        yield

    def query_side(self):
        for r in range(0, self.rows, STEP):
            gated = self.xs[TAPS + r : TAPS + r + STEP].astype(F32)
            filtered = own_groups(self.prod_f, r, STEP) + self.skip * gated
            self.out[r : r + STEP] = (self.act_q[r : r + STEP] * filtered).astype(BF16)
            grad = self.g[r : r + STEP].astype(F32) * weight_of(self.rep[r : r + STEP])
            grads = (grad * filtered).astype(BF16)
            self.gq[r : r + STEP] = grads
            short_sums(self.sums[0], grads, self.qf, EDGE + r)
            yield

    def key_value_side(self):
        for r in range(0, self.rows, STEP):
            scaled = self.gs[r : r + STEP].astype(F32)
            grad_gated = self.skip * scaled + own_groups(self.prod_b, r, STEP)
            grads = (grad_gated * self.act_v[r : r + STEP]).astype(BF16)
            self.gk[r : r + STEP] = grads
            short_sums(self.sums[1], grads, self.kf, EDGE + r)
            grads = (grad_gated * self.act_k[r : r + STEP]).astype(BF16)
            self.gv[r : r + STEP] = grads
            short_sums(self.sums[2], grads, self.vf, EDGE + r)
            yield

    def diagonals(self):
        sub = lax.broadcasted_iota(jnp.int32, (8, LANES), 0)
        lane = lax.broadcasted_iota(jnp.int32, (8, LANES), 1)
        prod = self.prod_p
        for n in range(PER_TILE):
            total = jnp.zeros((8, LANES), F32)
            for m in range(TAPS // 8):
                r = n * TAPS + m * 8
                ring = jnp.where(
                    lane >= sub + m * 8, prod[r : r + 8, :LANES], prod[r : r + 8, LANES:]
                )
                total = total + (pltpu.roll(ring, LANES - 8 * m, 1) if m else ring)
            self.diag[n * 8 : n * 8 + 8] = total
            if n % 2:
                yield
        lines = self.diag[pl.ds(0, PER_TILE, stride=8)]
        for r in range(1, 8):
            row = self.diag[pl.ds(r, PER_TILE, stride=8)]
            lines = lines + pltpu.roll(row, LANES - r, 1)
        self.part[:PER_TILE] = lines

    def finish(self):
        self.heads[:EDGE] = self.gq[:EDGE]
        self.heads[EDGE : 2 * EDGE] = self.gk[:EDGE]
        self.heads[2 * EDGE :] = self.gv[:EDGE]
        every = self.sums[0] + self.sums[1] + self.sums[2] + [self.skip_sum]
        lines = [jnp.sum(one, axis=0, keepdims=True) for one in every]
        lines.append(jnp.zeros((PART_ROWS - PER_TILE - len(lines), LANES), F32))
        self.part[PER_TILE:] = jnp.concatenate(lines, axis=0)
        yield


def main_kernel(
    ids, q, k, v, g, taps_ref, skip_ref, fwd, bwd, from_left, from_right,
    out, gq, gk, gv, heads, part, rep, *scratch,
):
    @pl.when(pl.program_id(0) == 0)
    def _():
        mark_repeats(ids, rep)

    each = len(scratch) // PER_STEP
    tiles = []
    for lt in range(PER_STEP):
        ls = slice(lt * LANES, (lt + 1) * LANES)
        tables = slice(lt * PER_TILE, (lt + 1) * PER_TILE)
        refs = [ref.at[:, ls] for ref in (q, k, v, g)]
        refs += [fwd.at[tables], bwd.at[tables]]
        refs += [ref.at[:, ls] for ref in (from_left, from_right, out, gq, gk, gv, heads)]
        refs += [part.at[pl.program_id(0) * PER_STEP + lt]]
        own = scratch[lt * each : (lt + 1) * each]
        tiles.append(Tile(refs, taps_ref[:, :, ls], skip_ref[:, ls], rep, own))
    together(tiles[0].activations())
    for n, tile in enumerate(tiles):
        following = tiles[n + 1 : n + 2]
        if n == 0:
            together(tile.forward_products(), *[t.activations() for t in following])
        together(tile.backward_products(), tile.query_side())
        together(tile.pair_products(), tile.key_value_side())
        together(
            tile.diagonals(), *[t.forward_products() for t in following], tile.finish()
        )


def back_kernel(grads, heads, taps_ref, result, frame):
    rows = grads.shape[0]
    step = 64
    for lt in range(grads.shape[1] // LANES):
        ls = slice(lt * LANES, (lt + 1) * LANES)
        frame[:rows] = grads[:, ls].astype(F32)
        frame[rows:] = heads[:, ls].astype(F32)
        for r in range(0, rows, step):
            total = taps_ref[0, 0:1, ls] * frame[pl.ds(r, step)]
            for j in range(1, SHORT):
                total = total + taps_ref[0, j : j + 1, ls] * frame[pl.ds(r + j, step)]
            result[r : r + step, ls] = total.astype(BF16)


def params(limit=60):
    return pltpu.CompilerParams(
        dimension_semantics=("arbitrary",), vmem_limit_bytes=limit * MIB
    )


def columns(rows, width):
    return pl.BlockSpec((rows, width), lambda i: (0, i))


def fixed(shape):
    return pl.BlockSpec(shape, lambda i: (0,) * len(shape))


def along_tile(count, width):
    return pl.BlockSpec((3, count, width), lambda i: (0, 0, i))


def make_edges(ids, q, k, v, g, taps):
    rows, channels = q.shape
    width = 1024
    first = pl.BlockSpec((TAPS, width), lambda i: (0, i))
    last = pl.BlockSpec((TAPS, width), lambda i: (rows // TAPS - 1, i))
    ahead = pl.BlockSpec((EDGE, width), lambda i: ((rows - TAPS) // EDGE - 1, i))
    tail = pl.BlockSpec((EDGE, width), lambda i: (rows // EDGE - 1, i))
    return pl.pallas_call(
        edges_kernel,
        grid=(channels // width,),
        in_specs=[pl.BlockSpec(memory_space=pltpu.SMEM), first, first, ahead, last, ahead, last]
        + [tail, along_tile(SHORT, width)],
        out_specs=[columns(TAPS + 2 * EDGE, width), columns(TAPS + 2 * EDGE, width)],
        out_shape=[
            jax.ShapeDtypeStruct((TAPS + 2 * EDGE, channels), BF16),
            jax.ShapeDtypeStruct((TAPS + 2 * EDGE, channels), BF16),
        ],
        scratch_shapes=[
            pltpu.VMEM((TAPS + EDGE, LANES), F32),
            pltpu.VMEM((TAPS + EDGE, LANES), F32),
            pltpu.VMEM((TAPS, LANES), F32),
            pltpu.VMEM((rows, LANES), F32),
        ],
        compiler_params=params(),
        name="edges",
    )(ids, q, g, k, k, v, v, q, taps)


def make_tables(long_filter):
    groups = long_filter.shape[0]
    wide = pl.BlockSpec((PER_TILE, TAPS, 2 * TAPS), lambda i: (i, 0, 0))
    return pl.pallas_call(
        tables_kernel,
        grid=(groups // PER_TILE,),
        in_specs=[fixed(long_filter.shape)],
        out_specs=[wide, wide],
        out_shape=[jax.ShapeDtypeStruct((groups, TAPS, 2 * TAPS), BF16)] * 2,
        scratch_shapes=[pltpu.VMEM((groups, TAPS), F32)] * 2,
        compiler_params=params(),
        cost_estimate=pl.CostEstimate(
            flops=0, bytes_accessed=32 * groups * TAPS * TAPS, transcendentals=0
        ),
        name="tables",
    )(long_filter)


def make_main(ids, q, k, v, g, taps, skip, fwd, bwd, from_left, from_right):
    rows, channels = q.shape
    tiles = channels // LANES
    wide = pl.BlockSpec((PER_STEP * PER_TILE, TAPS, 2 * TAPS), lambda i: (i, 0, 0))
    big = jax.ShapeDtypeStruct((rows, channels), BF16)
    return pl.pallas_call(
        main_kernel,
        grid=(tiles // PER_STEP,),
        in_specs=[pl.BlockSpec(memory_space=pltpu.SMEM)]
        + [columns(rows, WIDE)] * 4
        + [along_tile(SHORT, WIDE), columns(1, WIDE), wide, wide]
        + [columns(from_left.shape[0], WIDE), columns(from_right.shape[0], WIDE)],
        out_specs=[columns(rows, WIDE)] * 4
        + [columns(3 * EDGE, WIDE), pl.BlockSpec(memory_space=pltpu.VMEM)],
        out_shape=[big] * 4
        + [
            jax.ShapeDtypeStruct((3 * EDGE, channels), BF16),
            pltpu.VMEM((tiles, PART_ROWS, LANES), F32),
        ],
        scratch_shapes=[pltpu.VMEM((rows, LANES), F32)]
        + PER_STEP
        * [
            pltpu.VMEM((rows + 2 * EDGE, LANES), F32),
            pltpu.VMEM((rows + EDGE, LANES), F32),
            pltpu.VMEM((rows + EDGE, LANES), F32),
            pltpu.VMEM((rows + TAPS, LANES), BF16),
            pltpu.VMEM((rows + TAPS, LANES), BF16),
            pltpu.VMEM((rows, LANES), F32),
            pltpu.VMEM((rows, LANES), F32),
            pltpu.VMEM((rows, LANES), F32),
            pltpu.VMEM((PER_TILE * TAPS, 2 * TAPS), F32),
            pltpu.VMEM((PER_TILE * TAPS, 2 * TAPS), F32),
            pltpu.VMEM((PER_TILE * TAPS, 2 * TAPS), F32),
            pltpu.VMEM((PER_TILE * 8, LANES), F32),
        ],
        compiler_params=params(),
        name="main",
    )(ids, q, k, v, g, taps, skip, fwd, bwd, from_left, from_right)


def make_back(which, grads, heads, taps):
    rows, channels = grads.shape
    width = 1024
    return pl.pallas_call(
        back_kernel,
        grid=(channels // width,),
        in_specs=[
            columns(rows, width),
            pl.BlockSpec((EDGE, width), lambda i: (which, i)),
            pl.BlockSpec((1, SHORT, width), lambda i: (which, 0, i)),
        ],
        out_specs=columns(rows, width),
        out_shape=jax.ShapeDtypeStruct((rows, channels), BF16),
        scratch_shapes=[pltpu.VMEM((rows + EDGE, LANES), F32)],
        compiler_params=params(),
        cost_estimate=pl.CostEstimate(
            flops=14 * rows * channels, bytes_accessed=8 * rows * channels, transcendentals=0
        ),
        name="back",
    )(grads, heads, taps)


def last_kernel(scale, which, half, other, long_grad, skip_grad, short_grad):
    mine = which[0]
    tiles = 2 * half.shape[0] // PART_ROWS
    for tile in range(tiles):
        side, at = divmod(tile, tiles // 2)
        rows = slice(at * PART_ROWS, (at + 1) * PART_ROWS)
        both = jnp.where(mine == side, half[rows], other[rows]) * scale
        ls = slice(tile * LANES, (tile + 1) * LANES)
        long_grad[tile * PER_TILE : (tile + 1) * PER_TILE] = both[:PER_TILE]
        for i in range(3):
            first = PER_TILE + i * SHORT
            short_grad[i, :, ls] = both[first : first + SHORT]
        skip_grad[ls] = both[PER_TILE + 3 * SHORT]


def make_last(half, other, which, scale):
    tiles = 2 * half.shape[0] // PART_ROWS
    channels = tiles * LANES
    return pl.pallas_call(
        functools.partial(last_kernel, scale),
        in_specs=[pl.BlockSpec(memory_space=pltpu.SMEM)]
        + [pl.BlockSpec(memory_space=pltpu.VMEM)] * 2,
        out_specs=[pl.BlockSpec(memory_space=pltpu.VMEM)] * 3,
        out_shape=[
            jax.ShapeDtypeStruct((tiles * PER_TILE, TAPS), F32),
            jax.ShapeDtypeStruct((channels,), F32),
            jax.ShapeDtypeStruct((3, SHORT, channels), F32),
        ],
        compiler_params=pltpu.CompilerParams(vmem_limit_bytes=4 * MIB),
        name="last",
    )(which.reshape(1).astype(jnp.int32), half, other)


def from_behind(value, steps):
    count = lax.axis_size("seg") * lax.axis_size("ctx")
    first, last = max(0, -steps), min(count, count - steps)
    return lax.ppermute(value, AXES, [(s, s + steps) for s in range(first, last)])


def swap(value, mask):
    count = lax.axis_size("seg") * lax.axis_size("ctx")
    return lax.ppermute(value, AXES, [(s, s ^ mask) for s in range(count)])


def joined(value, masks):
    got = [value] + [swap(value, mask) for mask in masks]
    while len(got) > 1:
        got = [one + other for one, other in zip(got[::2], got[1::2])]
    return got[0]


def ring_masks(size):
    masks = []
    span = 1
    while span < size:
        masks.append(span if 2 * span < size or size == 2 else span + span // 2)
        span *= 2
    return masks


def total_over_all(value, work):
    ctx = lax.axis_size("ctx")
    seg = lax.axis_size("seg")
    me = lax.axis_index("seg") * ctx + lax.axis_index("ctx")
    cores = 2
    along = 1
    while along * along * cores < seg:
        along *= 2
    halving = [ctx, cores * ctx]
    doubling = [cores * ctx * m for m in ring_masks(along)]
    doubling += [cores * ctx * along * m for m in ring_masks(seg // (cores * along))]
    doubling = [(m,) for m in doubling if m not in halving]
    near = ring_masks(ctx)
    doubling += [(1, 2, 3)] if len(near) > 1 else [(m,) for m in near]
    doubling += [(m,) for m in near[2:]]
    mine = []
    done = []
    pending = list(work)
    for mask in halving:
        half = value.shape[0] // 2
        high = ((me // mask) % 2) == 1
        if mask != ctx:
            high = high ^ (((me // (2 * mask)) % 2) == 1)
        low_part, high_part = value[:half], value[half:]
        mine.append(high)
        got = swap(jnp.where(high, low_part, high_part), mask)
        value = jnp.where(high, high_part, low_part) + got
    for n, masks in enumerate(doubling):
        job = pending.pop(0) if pending and n >= 1 else None
        if job is None:
            value = joined(value, masks)
            continue
        run, inputs = job
        value, inputs = lax.optimization_barrier((value, inputs))
        value, result = lax.optimization_barrier((joined(value, masks), run(*inputs)))
        done.append(result)
    done += [run(*inputs) for run, inputs in pending]
    for mask, high in zip(halving[:0:-1], mine[:0:-1]):
        got = swap(value, mask)
        value = jnp.where(
            high, jnp.concatenate([got, value]), jnp.concatenate([value, got])
        )
    return value, swap(value, halving[0]), mine[0], done


def per_device(
    token_ids, query_in, key_in, value_in, short_filters, long_filter, skip_gain, out_grad
):
    length, channels = query_in.shape
    tiles = channels // LANES
    to_right, to_left = make_edges(
        token_ids, query_in, key_in, value_in, out_grad, short_filters
    )
    from_left = from_behind(to_right, 1)
    from_right = from_behind(to_left, -1)
    fwd, bwd = make_tables(long_filter)
    out, gq, gk, gv, heads, part = make_main(
        token_ids, query_in, key_in, value_in, out_grad, short_filters,
        skip_gain.reshape(1, channels), fwd, bwd, from_left, from_right,
    )
    next_heads = from_behind(heads, -1)
    jobs = [
        (functools.partial(make_back, i), (grads, next_heads, short_filters))
        for i, grads in enumerate((gq, gk, gv))
    ]
    half, other, which, (grad_query, grad_key, grad_value) = total_over_all(
        part.reshape(tiles * PART_ROWS, LANES), jobs
    )
    norm_scale = float(length * lax.axis_size("seg") * lax.axis_size("ctx")) ** (-0.5)
    grad_long, grad_skip, grad_short = make_last(half, other, which, norm_scale)
    return out, grad_query, grad_key, grad_value, grad_long, grad_skip, grad_short


def solution(mesh):
    sharded = P(("seg", "ctx"), None)
    return jax.shard_map(
        per_device,
        mesh=mesh,
        in_specs=(P(("seg", "ctx")), sharded, sharded, sharded, P(), P(), P(), sharded),
        out_specs=(sharded, sharded, sharded, sharded, P(), P(), P()),
        check_vma=False,
    )
```

```python
import functools

import jax
import jax.numpy as jnp
from jax import lax
from jax.experimental import pallas as pl
from jax.experimental.pallas import tpu as pltpu
from jax.sharding import PartitionSpec as P

GROUP = 16
TAPS = 128
SHORT = 7
LANES = 128
PER_TILE = LANES // GROUP
EDGE = 16
RUN = 32
PART_ROWS = 32
PER_STEP = 2
WIDE = PER_STEP * LANES
STEP = 64
TAIL = 8
AXES = ("seg", "ctx")
MIB = 1024 * 1024
F32 = jnp.float32
BF16 = jnp.bfloat16


def causal(frame, which, taps, start, count):
    total = taps[which, 0:1] * frame[pl.ds(start, count)]
    for j in range(1, SHORT):
        total = total + taps[which, j : j + 1] * frame[pl.ds(start - j, count)]
    return total


def weight_of(repeat):
    return jnp.where(repeat > 0.5, F32(0.1), F32(1.0))


def mark_repeats(ids, marks):
    rows = marks.shape[0]
    row = lax.broadcasted_iota(jnp.int32, (RUN, LANES), 0)

    def mark(at):
        return jnp.full((RUN, LANES), (ids[at] >= 97).astype(F32))

    for r in range(0, rows, RUN):
        run = mark(r + 1)
        if r == 0:
            run = jnp.where(row == 0, mark(0), run)
        if r + RUN == rows:
            run = jnp.where(row == RUN - 1, mark(rows - 1), run)
        marks[r : r + RUN] = run


def edges_kernel(
    ids, q, g, k_edge, k, v_edge, v, q_tail, taps_ref, right, left, kf, vf, qf, rep
):
    @pl.when(pl.program_id(0) == 0)
    def _():
        mark_repeats(ids, rep)

    for lt in range(q.shape[1] // LANES):
        ls = slice(lt * LANES, (lt + 1) * LANES)
        taps = taps_ref[:, :, ls]
        kf[:EDGE] = k_edge[:, ls].astype(F32)
        vf[:EDGE] = v_edge[:, ls].astype(F32)
        kf[EDGE:] = k[:, ls].astype(F32)
        vf[EDGE:] = v[:, ls].astype(F32)
        qf[...] = q[:, ls].astype(F32)
        for r in range(0, TAPS, 64):
            act_k = causal(kf, 1, taps, EDGE + r, 64)
            act_v = causal(vf, 2, taps, EDGE + r, 64)
            right[r : r + 64, ls] = (act_k * act_v).astype(BF16)
        tails = [kf[TAPS + EDGE - TAIL :], vf[TAPS + EDGE - TAIL :]]
        tails += [q_tail[:, ls].astype(F32)[EDGE - TAIL :], jnp.zeros((TAIL, LANES), F32)]
        right[TAPS:, ls] = jnp.concatenate(tails, axis=0).astype(BF16)
        for r, count in ((EDGE, 48), (EDGE + 48, 64)):
            act_q = causal(qf, 0, taps, r, count)
            grad = g[r : r + count, ls].astype(F32) * weight_of(rep[r : r + count])
            left[r - EDGE : r - EDGE + count, ls] = (grad * act_q).astype(BF16)
        left[TAPS - EDGE : TAPS, ls] = q[:EDGE, ls]
        left[TAPS : TAPS + EDGE, ls] = g[:EDGE, ls]
        left[TAPS + EDGE : TAPS + 2 * EDGE, ls] = rep[:EDGE].astype(BF16)


def tables_kernel(taps, fwd, bwd, plain, backwards):
    row = lax.broadcasted_iota(jnp.int32, (TAPS, TAPS), 0)
    col = lax.broadcasted_iota(jnp.int32, (TAPS, TAPS), 1)
    tile = pl.program_id(0)

    @pl.when(tile == 0)
    def _():
        mirror = ((row + col == TAPS) | ((row == 0) & (col == 0))).astype(BF16)
        plain[...] = taps[...].astype(F32)
        backwards[...] = jnp.dot(taps[...], mirror, preferred_element_type=F32)

    first = pl.multiple_of(tile * PER_TILE, PER_TILE)
    plain_rows = plain[pl.ds(first, PER_TILE)]
    backward_rows = backwards[pl.ds(first, PER_TILE)]

    def rings(source, g):
        spread = jnp.broadcast_to(source[g : g + 1], (TAPS, TAPS))
        return pltpu.roll(spread, 0, 1, stride=1, stride_axis=0)

    for g in range(PER_TILE):
        ring = rings(backward_rows, g)
        fwd[g, :, :TAPS] = jnp.where(col > row, ring, 0.0).astype(BF16)
        fwd[g, :, TAPS:] = jnp.where(col <= row, ring, 0.0).astype(BF16)
        ring = rings(plain_rows, g)
        bwd[g, :, :TAPS] = jnp.where(col >= row, ring, 0.0).astype(BF16)
        bwd[g, :, TAPS:] = jnp.where(col < row, ring, 0.0).astype(BF16)


def together(*jobs):
    jobs = list(jobs)
    while jobs:
        for job in list(jobs):
            if next(job, jobs) is jobs:
                jobs.remove(job)


def short_sums(sums, grads, frame, start):
    wide = grads.astype(F32)
    count = wide.shape[0]
    for j in range(SHORT):
        both = wide * frame[pl.ds(start - j, count)]
        sums[j] = sums[j] + jnp.sum(both.reshape(count // 8, 8, LANES), axis=0)


def own_groups(prod, r, count):
    block, at = divmod(r, TAPS)
    ls = slice(block * LANES, (block + 1) * LANES)
    lane = lax.broadcasted_iota(jnp.int32, (count, LANES), 1) // GROUP
    total = prod[at : at + count, ls]
    for n in range(1, PER_TILE):
        total = jnp.where(lane == n, prod[n * TAPS + at : n * TAPS + at + count, ls], total)
    return total


class Tile:
    def __init__(self, refs, taps, skip, rep, scratch):
        (self.q, self.k, self.v, self.g, self.fwd, self.bwd, self.from_left, self.from_right,
         self.out, self.gq, self.gk, self.gv, self.heads, self.part) = refs
        (self.qf, self.kf, self.vf, self.xs, self.gs, self.act_q, self.act_k, self.act_v,
         self.prod_p, self.prod_f, self.prod_b, self.diag) = scratch
        self.taps, self.skip, self.rep = taps, skip, rep
        self.rows = self.q.shape[0]
        self.sums = [[jnp.zeros((8, LANES), F32)] * SHORT for _ in range(3)]
        self.skip_sum = jnp.zeros((8, LANES), F32)

    def activations(self):
        rows, taps, qf, kf, vf = self.rows, self.taps, self.qf, self.kf, self.vf
        from_left, from_right = self.from_left, self.from_right
        qf[EDGE : EDGE + rows] = self.q[...].astype(F32)
        kf[EDGE : EDGE + rows] = self.k[...].astype(F32)
        vf[EDGE : EDGE + rows] = self.v[...].astype(F32)
        tails = from_left[TAPS:].astype(F32)
        kf[EDGE - TAIL : EDGE] = tails[:TAIL]
        vf[EDGE - TAIL : EDGE] = tails[TAIL : 2 * TAIL]
        qf[EDGE - TAIL : EDGE] = tails[2 * TAIL : 3 * TAIL]
        qf[EDGE + rows :] = from_right[TAPS - EDGE : TAPS].astype(F32)
        self.xs[:TAPS] = from_left[:TAPS]
        self.gs[rows + EDGE :] = from_right[: TAPS - EDGE]
        grad = from_right[TAPS : TAPS + EDGE].astype(F32) * weight_of(
            from_right[TAPS + EDGE : TAPS + 2 * EDGE].astype(F32)
        )
        a_q = causal(qf, 0, taps, EDGE + rows, EDGE)
        self.gs[rows : rows + EDGE] = (grad * a_q).astype(BF16)
        for r in range(0, rows, STEP):
            a_q = causal(qf, 0, taps, EDGE + r, STEP)
            a_k = causal(kf, 1, taps, EDGE + r, STEP)
            a_v = causal(vf, 2, taps, EDGE + r, STEP)
            self.act_q[r : r + STEP] = a_q
            self.act_k[r : r + STEP] = a_k
            self.act_v[r : r + STEP] = a_v
            gated = (a_k * a_v).astype(BF16)
            self.xs[TAPS + r : TAPS + r + STEP] = gated
            grad = self.g[r : r + STEP].astype(F32) * weight_of(self.rep[r : r + STEP])
            scaled = (grad * a_q).astype(BF16)
            self.gs[r : r + STEP] = scaled
            both = scaled.astype(F32) * gated.astype(F32)
            self.skip_sum = self.skip_sum + jnp.sum(both.reshape(STEP // 8, 8, LANES), axis=0)
            yield

    def window(self, rows_of):
        return jnp.concatenate([rows_of[: 2 * TAPS], rows_of[TAPS:]], axis=1)

    def filter_products(self, table, rows_of, prod):
        whole = table[...].reshape(PER_TILE * TAPS, 2 * TAPS)
        prod[...] = jnp.dot(whole, self.window(rows_of), preferred_element_type=F32)
        yield

    def forward_products(self):
        return self.filter_products(self.fwd, self.xs, self.prod_f)

    def backward_products(self):
        return self.filter_products(self.bwd, self.gs, self.prod_b)

    def pair_products(self):
        windows = self.window(self.gs)
        own_x = jnp.concatenate([self.xs[TAPS : 2 * TAPS], self.xs[2 * TAPS :]], axis=1)
        lane = lax.broadcasted_iota(jnp.int32, own_x.shape, 1) % LANES // GROUP
        masked = jnp.concatenate(
            [jnp.where(lane == n, own_x, jnp.zeros_like(own_x)) for n in range(PER_TILE)],
            axis=0,
        )
        self.prod_p[...] = lax.dot_general(
            masked, windows, (((1,), (1,)), ((), ())), preferred_element_type=F32
        )
        yield

    def query_side(self):
        for r in range(0, self.rows, STEP):
            gated = self.xs[TAPS + r : TAPS + r + STEP].astype(F32)
            filtered = own_groups(self.prod_f, r, STEP) + self.skip * gated
            self.out[r : r + STEP] = (self.act_q[r : r + STEP] * filtered).astype(BF16)
            grad = self.g[r : r + STEP].astype(F32) * weight_of(self.rep[r : r + STEP])
            grads = (grad * filtered).astype(BF16)
            self.gq[r : r + STEP] = grads
            short_sums(self.sums[0], grads, self.qf, EDGE + r)
            yield

    def key_value_side(self):
        for r in range(0, self.rows, STEP):
            scaled = self.gs[r : r + STEP].astype(F32)
            grad_gated = self.skip * scaled + own_groups(self.prod_b, r, STEP)
            grads = (grad_gated * self.act_v[r : r + STEP]).astype(BF16)
            self.gk[r : r + STEP] = grads
            short_sums(self.sums[1], grads, self.kf, EDGE + r)
            grads = (grad_gated * self.act_k[r : r + STEP]).astype(BF16)
            self.gv[r : r + STEP] = grads
            short_sums(self.sums[2], grads, self.vf, EDGE + r)
            yield

    def diagonals(self):
        sub = lax.broadcasted_iota(jnp.int32, (8, LANES), 0)
        lane = lax.broadcasted_iota(jnp.int32, (8, LANES), 1)
        prod = self.prod_p
        for n in range(PER_TILE):
            total = jnp.zeros((8, LANES), F32)
            for m in range(TAPS // 8):
                r = n * TAPS + m * 8
                ring = jnp.where(
                    lane >= sub + m * 8, prod[r : r + 8, :LANES], prod[r : r + 8, LANES:]
                )
                total = total + (pltpu.roll(ring, LANES - 8 * m, 1) if m else ring)
            self.diag[n * 8 : n * 8 + 8] = total
            if n % 2:
                yield
        lines = self.diag[pl.ds(0, PER_TILE, stride=8)]
        for r in range(1, 8):
            row = self.diag[pl.ds(r, PER_TILE, stride=8)]
            lines = lines + pltpu.roll(row, LANES - r, 1)
        self.part[:PER_TILE] = lines

    def finish(self):
        self.heads[:EDGE] = self.gq[:EDGE]
        self.heads[EDGE : 2 * EDGE] = self.gk[:EDGE]
        self.heads[2 * EDGE :] = self.gv[:EDGE]
        every = self.sums[0] + self.sums[1] + self.sums[2] + [self.skip_sum]
        lines = [jnp.sum(one, axis=0, keepdims=True) for one in every]
        lines.append(jnp.zeros((PART_ROWS - PER_TILE - len(lines), LANES), F32))
        self.part[PER_TILE:] = jnp.concatenate(lines, axis=0)
        yield


def main_kernel(
    ids, q, k, v, g, taps_ref, skip_ref, fwd, bwd, from_left, from_right,
    out, gq, gk, gv, heads, part, rep, *scratch,
):
    @pl.when(pl.program_id(0) == 0)
    def _():
        mark_repeats(ids, rep)

    each = len(scratch) // PER_STEP
    tiles = []
    for lt in range(PER_STEP):
        ls = slice(lt * LANES, (lt + 1) * LANES)
        tables = slice(lt * PER_TILE, (lt + 1) * PER_TILE)
        refs = [ref.at[:, ls] for ref in (q, k, v, g)]
        refs += [fwd.at[tables], bwd.at[tables]]
        refs += [ref.at[:, ls] for ref in (from_left, from_right, out, gq, gk, gv, heads)]
        refs += [part.at[pl.program_id(0) * PER_STEP + lt]]
        own = scratch[lt * each : (lt + 1) * each]
        tiles.append(Tile(refs, taps_ref[:, :, ls], skip_ref[:, ls], rep, own))
    together(tiles[0].activations())
    for n, tile in enumerate(tiles):
        following = tiles[n + 1 : n + 2]
        if n == 0:
            together(tile.forward_products(), *[t.activations() for t in following])
        together(tile.backward_products(), tile.query_side())
        together(tile.pair_products(), tile.key_value_side())
        together(
            tile.diagonals(), *[t.forward_products() for t in following], tile.finish()
        )


def back_kernel(grads, heads, taps_ref, result, frame):
    rows = grads.shape[0]
    step = 64
    for lt in range(grads.shape[1] // LANES):
        ls = slice(lt * LANES, (lt + 1) * LANES)
        frame[:rows] = grads[:, ls].astype(F32)
        frame[rows:] = heads[:, ls].astype(F32)
        for r in range(0, rows, step):
            total = taps_ref[0, 0:1, ls] * frame[pl.ds(r, step)]
            for j in range(1, SHORT):
                total = total + taps_ref[0, j : j + 1, ls] * frame[pl.ds(r + j, step)]
            result[r : r + step, ls] = total.astype(BF16)


def params(limit=60):
    return pltpu.CompilerParams(
        dimension_semantics=("arbitrary",), vmem_limit_bytes=limit * MIB
    )


def columns(rows, width):
    return pl.BlockSpec((rows, width), lambda i: (0, i))


def fixed(shape):
    return pl.BlockSpec(shape, lambda i: (0,) * len(shape))


def along_tile(count, width):
    return pl.BlockSpec((3, count, width), lambda i: (0, 0, i))


def make_edges(ids, q, k, v, g, taps):
    rows, channels = q.shape
    width = 1024
    first = pl.BlockSpec((TAPS, width), lambda i: (0, i))
    last = pl.BlockSpec((TAPS, width), lambda i: (rows // TAPS - 1, i))
    ahead = pl.BlockSpec((EDGE, width), lambda i: ((rows - TAPS) // EDGE - 1, i))
    tail = pl.BlockSpec((EDGE, width), lambda i: (rows // EDGE - 1, i))
    return pl.pallas_call(
        edges_kernel,
        grid=(channels // width,),
        in_specs=[pl.BlockSpec(memory_space=pltpu.SMEM), first, first, ahead, last, ahead, last]
        + [tail, along_tile(SHORT, width)],
        out_specs=[columns(TAPS + 2 * EDGE, width), columns(TAPS + 2 * EDGE, width)],
        out_shape=[
            jax.ShapeDtypeStruct((TAPS + 2 * EDGE, channels), BF16),
            jax.ShapeDtypeStruct((TAPS + 2 * EDGE, channels), BF16),
        ],
        scratch_shapes=[
            pltpu.VMEM((TAPS + EDGE, LANES), F32),
            pltpu.VMEM((TAPS + EDGE, LANES), F32),
            pltpu.VMEM((TAPS, LANES), F32),
            pltpu.VMEM((rows, LANES), F32),
        ],
        compiler_params=params(),
        name="edges",
    )(ids, q, g, k, k, v, v, q, taps)


def make_tables(long_filter):
    groups = long_filter.shape[0]
    wide = pl.BlockSpec((PER_TILE, TAPS, 2 * TAPS), lambda i: (i, 0, 0))
    return pl.pallas_call(
        tables_kernel,
        grid=(groups // PER_TILE,),
        in_specs=[fixed(long_filter.shape)],
        out_specs=[wide, wide],
        out_shape=[jax.ShapeDtypeStruct((groups, TAPS, 2 * TAPS), BF16)] * 2,
        scratch_shapes=[pltpu.VMEM((groups, TAPS), F32)] * 2,
        compiler_params=params(),
        cost_estimate=pl.CostEstimate(
            flops=0, bytes_accessed=32 * groups * TAPS * TAPS, transcendentals=0
        ),
        name="tables",
    )(long_filter)


def make_main(ids, q, k, v, g, taps, skip, fwd, bwd, from_left, from_right):
    rows, channels = q.shape
    tiles = channels // LANES
    wide = pl.BlockSpec((PER_STEP * PER_TILE, TAPS, 2 * TAPS), lambda i: (i, 0, 0))
    big = jax.ShapeDtypeStruct((rows, channels), BF16)
    return pl.pallas_call(
        main_kernel,
        grid=(tiles // PER_STEP,),
        in_specs=[pl.BlockSpec(memory_space=pltpu.SMEM)]
        + [columns(rows, WIDE)] * 4
        + [along_tile(SHORT, WIDE), columns(1, WIDE), wide, wide]
        + [columns(from_left.shape[0], WIDE), columns(from_right.shape[0], WIDE)],
        out_specs=[columns(rows, WIDE)] * 4
        + [columns(3 * EDGE, WIDE), pl.BlockSpec(memory_space=pltpu.VMEM)],
        out_shape=[big] * 4
        + [
            jax.ShapeDtypeStruct((3 * EDGE, channels), BF16),
            pltpu.VMEM((tiles, PART_ROWS, LANES), F32),
        ],
        scratch_shapes=[pltpu.VMEM((rows, LANES), F32)]
        + PER_STEP
        * [
            pltpu.VMEM((rows + 2 * EDGE, LANES), F32),
            pltpu.VMEM((rows + EDGE, LANES), F32),
            pltpu.VMEM((rows + EDGE, LANES), F32),
            pltpu.VMEM((rows + TAPS, LANES), BF16),
            pltpu.VMEM((rows + TAPS, LANES), BF16),
            pltpu.VMEM((rows, LANES), F32),
            pltpu.VMEM((rows, LANES), F32),
            pltpu.VMEM((rows, LANES), F32),
            pltpu.VMEM((PER_TILE * TAPS, 2 * TAPS), F32),
            pltpu.VMEM((PER_TILE * TAPS, 2 * TAPS), F32),
            pltpu.VMEM((PER_TILE * TAPS, 2 * TAPS), F32),
            pltpu.VMEM((PER_TILE * 8, LANES), F32),
        ],
        compiler_params=params(),
        name="main",
    )(ids, q, k, v, g, taps, skip, fwd, bwd, from_left, from_right)


def make_back(which, grads, heads, taps):
    rows, channels = grads.shape
    width = 1024
    return pl.pallas_call(
        back_kernel,
        grid=(channels // width,),
        in_specs=[
            columns(rows, width),
            pl.BlockSpec((EDGE, width), lambda i: (which, i)),
            pl.BlockSpec((1, SHORT, width), lambda i: (which, 0, i)),
        ],
        out_specs=columns(rows, width),
        out_shape=jax.ShapeDtypeStruct((rows, channels), BF16),
        scratch_shapes=[pltpu.VMEM((rows + EDGE, LANES), F32)],
        compiler_params=params(),
        cost_estimate=pl.CostEstimate(
            flops=14 * rows * channels, bytes_accessed=8 * rows * channels, transcendentals=0
        ),
        name="back",
    )(grads, heads, taps)


def last_kernel(scale, which, half, other, long_grad, skip_grad, short_grad):
    mine = which[0]
    tiles = 2 * half.shape[0] // PART_ROWS
    for tile in range(tiles):
        side, at = divmod(tile, tiles // 2)
        rows = slice(at * PART_ROWS, (at + 1) * PART_ROWS)
        both = jnp.where(mine == side, half[rows], other[rows]) * scale
        ls = slice(tile * LANES, (tile + 1) * LANES)
        long_grad[tile * PER_TILE : (tile + 1) * PER_TILE] = both[:PER_TILE]
        for i in range(3):
            first = PER_TILE + i * SHORT
            short_grad[i, :, ls] = both[first : first + SHORT]
        skip_grad[ls] = both[PER_TILE + 3 * SHORT]


def make_last(half, other, which, scale):
    tiles = 2 * half.shape[0] // PART_ROWS
    channels = tiles * LANES
    return pl.pallas_call(
        functools.partial(last_kernel, scale),
        in_specs=[pl.BlockSpec(memory_space=pltpu.SMEM)]
        + [pl.BlockSpec(memory_space=pltpu.VMEM)] * 2,
        out_specs=[pl.BlockSpec(memory_space=pltpu.VMEM)] * 3,
        out_shape=[
            jax.ShapeDtypeStruct((tiles * PER_TILE, TAPS), F32),
            jax.ShapeDtypeStruct((channels,), F32),
            jax.ShapeDtypeStruct((3, SHORT, channels), F32),
        ],
        compiler_params=pltpu.CompilerParams(vmem_limit_bytes=4 * MIB),
        name="last",
    )(which.reshape(1).astype(jnp.int32), half, other)


def from_behind(value, steps):
    count = lax.axis_size("seg") * lax.axis_size("ctx")
    first, last = max(0, -steps), min(count, count - steps)
    return lax.ppermute(value, AXES, [(s, s + steps) for s in range(first, last)])


def swap(value, mask):
    count = lax.axis_size("seg") * lax.axis_size("ctx")
    return lax.ppermute(value, AXES, [(s, s ^ mask) for s in range(count)])


def joined(value, masks):
    got = [value] + [swap(value, mask) for mask in masks]
    while len(got) > 1:
        got = [one + other for one, other in zip(got[::2], got[1::2])]
    return got[0]


def ring_masks(size):
    masks = []
    span = 1
    while span < size:
        masks.append(span if 2 * span < size or size == 2 else span + span // 2)
        span *= 2
    return masks


def ring_steps(size):
    masks = ring_masks(size)
    return [(1, 2, 3)] + [(m,) for m in masks[2:]] if len(masks) > 1 else [(m,) for m in masks]


def total_over_all(value, work):
    ctx = lax.axis_size("ctx")
    seg = lax.axis_size("seg")
    me = lax.axis_index("seg") * ctx + lax.axis_index("ctx")
    cores = 2
    along = 1
    while along * along * cores < seg:
        along *= 2
    halving = [ctx, cores * ctx]
    x_unit, y_unit = cores * ctx, cores * ctx * along
    doubling = [(x_unit * m,) for m in ring_masks(along) if x_unit * m not in halving]
    doubling += [tuple(y_unit * m for m in step) for step in ring_steps(seg // (cores * along))]
    doubling += ring_steps(ctx)
    mine = []
    done = []
    pending = list(work)
    for mask in halving:
        half = value.shape[0] // 2
        high = ((me // mask) % 2) == 1
        if mask != ctx:
            high = high ^ (((me // (2 * mask)) % 2) == 1)
        low_part, high_part = value[:half], value[half:]
        mine.append(high)
        got = swap(jnp.where(high, low_part, high_part), mask)
        value = jnp.where(high, high_part, low_part) + got
    for n, masks in enumerate(doubling):
        job = pending.pop(0) if pending and n >= 1 else None
        if job is None:
            value = joined(value, masks)
            continue
        run, inputs = job
        value, inputs = lax.optimization_barrier((value, inputs))
        value, result = lax.optimization_barrier((joined(value, masks), run(*inputs)))
        done.append(result)
    done += [run(*inputs) for run, inputs in pending]
    for mask, high in zip(halving[:0:-1], mine[:0:-1]):
        got = swap(value, mask)
        value = jnp.where(
            high, jnp.concatenate([got, value]), jnp.concatenate([value, got])
        )
    return value, swap(value, halving[0]), mine[0], done


def per_device(
    token_ids, query_in, key_in, value_in, short_filters, long_filter, skip_gain, out_grad
):
    length, channels = query_in.shape
    tiles = channels // LANES
    to_right, to_left = make_edges(
        token_ids, query_in, key_in, value_in, out_grad, short_filters
    )
    from_left = from_behind(to_right, 1)
    from_right = from_behind(to_left, -1)
    fwd, bwd = make_tables(long_filter)
    out, gq, gk, gv, heads, part = make_main(
        token_ids, query_in, key_in, value_in, out_grad, short_filters,
        skip_gain.reshape(1, channels), fwd, bwd, from_left, from_right,
    )
    next_heads = from_behind(heads, -1)
    jobs = [
        (functools.partial(make_back, i), (grads, next_heads, short_filters))
        for i, grads in enumerate((gq, gk, gv))
    ]
    half, other, which, (grad_query, grad_key, grad_value) = total_over_all(
        part.reshape(tiles * PART_ROWS, LANES), jobs
    )
    norm_scale = float(length * lax.axis_size("seg") * lax.axis_size("ctx")) ** (-0.5)
    grad_long, grad_skip, grad_short = make_last(half, other, which, norm_scale)
    return out, grad_query, grad_key, grad_value, grad_long, grad_skip, grad_short


def solution(mesh):
    sharded = P(("seg", "ctx"), None)
    return jax.shard_map(
        per_device,
        mesh=mesh,
        in_specs=(P(("seg", "ctx")), sharded, sharded, sharded, P(), P(), P(), sharded),
        out_specs=(sharded, sharded, sharded, sharded, P(), P(), P()),
        check_vma=False,
    )
```

```python
import functools

import jax
import jax.numpy as jnp
from jax import lax
from jax.experimental import pallas as pl
from jax.experimental.pallas import tpu as pltpu
from jax.sharding import PartitionSpec as P

GROUP = 16
TAPS = 128
SHORT = 7
LANES = 128
PER_TILE = LANES // GROUP
EDGE = 16
RUN = 32
PART_ROWS = 32
PER_STEP = 2
WIDE = PER_STEP * LANES
STEP = 64
TAIL = 8
AXES = ("seg", "ctx")
MIB = 1024 * 1024
F32 = jnp.float32
BF16 = jnp.bfloat16


def causal(frame, which, taps, start, count):
    total = taps[which, 0:1] * frame[pl.ds(start, count)]
    for j in range(1, SHORT):
        total = total + taps[which, j : j + 1] * frame[pl.ds(start - j, count)]
    return total


def weight_of(repeat):
    return jnp.where(repeat > 0.5, F32(0.1), F32(1.0))


def mark_repeats(ids, marks):
    rows = marks.shape[0]
    row = lax.broadcasted_iota(jnp.int32, (RUN, LANES), 0)

    def mark(at):
        return jnp.full((RUN, LANES), (ids[at] >= 97).astype(F32))

    for r in range(0, rows, RUN):
        run = mark(r + 1)
        if r == 0:
            run = jnp.where(row == 0, mark(0), run)
        if r + RUN == rows:
            run = jnp.where(row == RUN - 1, mark(rows - 1), run)
        marks[r : r + RUN] = run


def edges_kernel(
    ids, q, g, k_edge, k, v_edge, v, q_tail, taps_ref, right, left, kf, vf, qf, rep
):
    @pl.when(pl.program_id(0) == 0)
    def _():
        mark_repeats(ids, rep)

    for lt in range(q.shape[1] // LANES):
        ls = slice(lt * LANES, (lt + 1) * LANES)
        taps = taps_ref[:, :, ls]
        kf[:EDGE] = k_edge[:, ls].astype(F32)
        vf[:EDGE] = v_edge[:, ls].astype(F32)
        kf[EDGE:] = k[:, ls].astype(F32)
        vf[EDGE:] = v[:, ls].astype(F32)
        qf[...] = q[:, ls].astype(F32)
        for r in range(0, TAPS, 64):
            act_k = causal(kf, 1, taps, EDGE + r, 64)
            act_v = causal(vf, 2, taps, EDGE + r, 64)
            right[r : r + 64, ls] = (act_k * act_v).astype(BF16)
        tails = [kf[TAPS + EDGE - TAIL :], vf[TAPS + EDGE - TAIL :]]
        tails += [q_tail[:, ls].astype(F32)[EDGE - TAIL :], jnp.zeros((TAIL, LANES), F32)]
        right[TAPS:, ls] = jnp.concatenate(tails, axis=0).astype(BF16)
        for r, count in ((EDGE, 48), (EDGE + 48, 64)):
            act_q = causal(qf, 0, taps, r, count)
            grad = g[r : r + count, ls].astype(F32) * weight_of(rep[r : r + count])
            left[r - EDGE : r - EDGE + count, ls] = (grad * act_q).astype(BF16)
        left[TAPS - EDGE : TAPS, ls] = q[:EDGE, ls]
        left[TAPS : TAPS + EDGE, ls] = g[:EDGE, ls]
        left[TAPS + EDGE : TAPS + 2 * EDGE, ls] = rep[:EDGE].astype(BF16)


def tables_kernel(taps, skip_in, fwd, bwd, skip, plain, backwards):
    row = lax.broadcasted_iota(jnp.int32, (TAPS, TAPS), 0)
    col = lax.broadcasted_iota(jnp.int32, (TAPS, TAPS), 1)
    tile = pl.program_id(0)

    @pl.when(tile == 0)
    def _():
        mirror = ((row + col == TAPS) | ((row == 0) & (col == 0))).astype(BF16)
        plain[...] = taps[...].astype(F32)
        backwards[...] = jnp.dot(taps[...], mirror, preferred_element_type=F32)
        skip[...] = skip_in[...]

    first = pl.multiple_of(tile * PER_TILE, PER_TILE)
    plain_rows = plain[pl.ds(first, PER_TILE)]
    backward_rows = backwards[pl.ds(first, PER_TILE)]

    def rings(source, g):
        spread = jnp.broadcast_to(source[g : g + 1], (TAPS, TAPS))
        return pltpu.roll(spread, 0, 1, stride=1, stride_axis=0)

    for g in range(PER_TILE):
        ring = rings(backward_rows, g)
        fwd[g, :, :TAPS] = jnp.where(col > row, ring, 0.0).astype(BF16)
        fwd[g, :, TAPS:] = jnp.where(col <= row, ring, 0.0).astype(BF16)
        ring = rings(plain_rows, g)
        bwd[g, :, :TAPS] = jnp.where(col >= row, ring, 0.0).astype(BF16)
        bwd[g, :, TAPS:] = jnp.where(col < row, ring, 0.0).astype(BF16)


def together(*jobs):
    jobs = list(jobs)
    while jobs:
        for job in list(jobs):
            if next(job, jobs) is jobs:
                jobs.remove(job)


def short_sums(sums, grads, frame, start):
    wide = grads.astype(F32)
    count = wide.shape[0]
    for j in range(SHORT):
        both = wide * frame[pl.ds(start - j, count)]
        sums[j] = sums[j] + jnp.sum(both.reshape(count // 8, 8, LANES), axis=0)


def own_groups(prod, r, count):
    block, at = divmod(r, TAPS)
    ls = slice(block * LANES, (block + 1) * LANES)
    lane = lax.broadcasted_iota(jnp.int32, (count, LANES), 1) // GROUP
    total = prod[at : at + count, ls]
    for n in range(1, PER_TILE):
        total = jnp.where(lane == n, prod[n * TAPS + at : n * TAPS + at + count, ls], total)
    return total


class Tile:
    def __init__(self, refs, taps, skip, rep, scratch):
        (self.q, self.k, self.v, self.g, self.fwd, self.bwd, self.from_left, self.from_right,
         self.out, self.gq, self.gk, self.gv, self.heads, self.part) = refs
        (self.qf, self.kf, self.vf, self.xs, self.gs, self.act_q, self.act_k, self.act_v,
         self.prod_p, self.prod_f, self.prod_b, self.diag) = scratch
        self.taps, self.skip, self.rep = taps, skip, rep
        self.rows = self.q.shape[0]
        self.sums = [[jnp.zeros((8, LANES), F32)] * SHORT for _ in range(3)]
        self.skip_sum = jnp.zeros((8, LANES), F32)

    def activations(self):
        rows, taps, qf, kf, vf = self.rows, self.taps, self.qf, self.kf, self.vf
        from_left, from_right = self.from_left, self.from_right
        qf[EDGE : EDGE + rows] = self.q[...].astype(F32)
        kf[EDGE : EDGE + rows] = self.k[...].astype(F32)
        vf[EDGE : EDGE + rows] = self.v[...].astype(F32)
        tails = from_left[TAPS:].astype(F32)
        kf[EDGE - TAIL : EDGE] = tails[:TAIL]
        vf[EDGE - TAIL : EDGE] = tails[TAIL : 2 * TAIL]
        qf[EDGE - TAIL : EDGE] = tails[2 * TAIL : 3 * TAIL]
        qf[EDGE + rows :] = from_right[TAPS - EDGE : TAPS].astype(F32)
        self.xs[:TAPS] = from_left[:TAPS]
        self.gs[rows + EDGE :] = from_right[: TAPS - EDGE]
        grad = from_right[TAPS : TAPS + EDGE].astype(F32) * weight_of(
            from_right[TAPS + EDGE : TAPS + 2 * EDGE].astype(F32)
        )
        a_q = causal(qf, 0, taps, EDGE + rows, EDGE)
        self.gs[rows : rows + EDGE] = (grad * a_q).astype(BF16)
        for r in range(0, rows, STEP):
            a_q = causal(qf, 0, taps, EDGE + r, STEP)
            a_k = causal(kf, 1, taps, EDGE + r, STEP)
            a_v = causal(vf, 2, taps, EDGE + r, STEP)
            self.act_q[r : r + STEP] = a_q
            self.act_k[r : r + STEP] = a_k
            self.act_v[r : r + STEP] = a_v
            gated = (a_k * a_v).astype(BF16)
            self.xs[TAPS + r : TAPS + r + STEP] = gated
            grad = self.g[r : r + STEP].astype(F32) * weight_of(self.rep[r : r + STEP])
            scaled = (grad * a_q).astype(BF16)
            self.gs[r : r + STEP] = scaled
            both = scaled.astype(F32) * gated.astype(F32)
            self.skip_sum = self.skip_sum + jnp.sum(both.reshape(STEP // 8, 8, LANES), axis=0)
            yield

    def window(self, rows_of):
        return jnp.concatenate([rows_of[: 2 * TAPS], rows_of[TAPS:]], axis=1)

    def filter_products(self, table, rows_of, prod):
        whole = table[...].reshape(PER_TILE * TAPS, 2 * TAPS)
        prod[...] = jnp.dot(whole, self.window(rows_of), preferred_element_type=F32)
        yield

    def forward_products(self):
        return self.filter_products(self.fwd, self.xs, self.prod_f)

    def backward_products(self):
        return self.filter_products(self.bwd, self.gs, self.prod_b)

    def pair_products(self):
        windows = self.window(self.gs)
        own_x = jnp.concatenate([self.xs[TAPS : 2 * TAPS], self.xs[2 * TAPS :]], axis=1)
        lane = lax.broadcasted_iota(jnp.int32, own_x.shape, 1) % LANES // GROUP
        masked = jnp.concatenate(
            [jnp.where(lane == n, own_x, jnp.zeros_like(own_x)) for n in range(PER_TILE)],
            axis=0,
        )
        self.prod_p[...] = lax.dot_general(
            masked, windows, (((1,), (1,)), ((), ())), preferred_element_type=F32
        )
        yield

    def query_side(self):
        for r in range(0, self.rows, STEP):
            gated = self.xs[TAPS + r : TAPS + r + STEP].astype(F32)
            filtered = own_groups(self.prod_f, r, STEP) + self.skip * gated
            self.out[r : r + STEP] = (self.act_q[r : r + STEP] * filtered).astype(BF16)
            grad = self.g[r : r + STEP].astype(F32) * weight_of(self.rep[r : r + STEP])
            grads = (grad * filtered).astype(BF16)
            self.gq[r : r + STEP] = grads
            short_sums(self.sums[0], grads, self.qf, EDGE + r)
            yield

    def key_value_side(self):
        for r in range(0, self.rows, STEP):
            scaled = self.gs[r : r + STEP].astype(F32)
            grad_gated = self.skip * scaled + own_groups(self.prod_b, r, STEP)
            grads = (grad_gated * self.act_v[r : r + STEP]).astype(BF16)
            self.gk[r : r + STEP] = grads
            short_sums(self.sums[1], grads, self.kf, EDGE + r)
            grads = (grad_gated * self.act_k[r : r + STEP]).astype(BF16)
            self.gv[r : r + STEP] = grads
            short_sums(self.sums[2], grads, self.vf, EDGE + r)
            yield

    def diagonals(self):
        sub = lax.broadcasted_iota(jnp.int32, (8, LANES), 0)
        lane = lax.broadcasted_iota(jnp.int32, (8, LANES), 1)
        prod = self.prod_p
        for n in range(PER_TILE):
            total = jnp.zeros((8, LANES), F32)
            for m in range(TAPS // 8):
                r = n * TAPS + m * 8
                ring = jnp.where(
                    lane >= sub + m * 8, prod[r : r + 8, :LANES], prod[r : r + 8, LANES:]
                )
                total = total + (pltpu.roll(ring, LANES - 8 * m, 1) if m else ring)
            self.diag[n * 8 : n * 8 + 8] = total
            if n % 2:
                yield
        lines = self.diag[pl.ds(0, PER_TILE, stride=8)]
        for r in range(1, 8):
            row = self.diag[pl.ds(r, PER_TILE, stride=8)]
            lines = lines + pltpu.roll(row, LANES - r, 1)
        self.part[:PER_TILE] = lines

    def finish(self):
        self.heads[:EDGE] = self.gq[:EDGE]
        self.heads[EDGE : 2 * EDGE] = self.gk[:EDGE]
        self.heads[2 * EDGE :] = self.gv[:EDGE]
        every = self.sums[0] + self.sums[1] + self.sums[2] + [self.skip_sum]
        lines = [jnp.sum(one, axis=0, keepdims=True) for one in every]
        lines.append(jnp.zeros((PART_ROWS - PER_TILE - len(lines), LANES), F32))
        self.part[PER_TILE:] = jnp.concatenate(lines, axis=0)
        yield


def main_kernel(
    ids, q, k, v, g, taps_ref, skip_ref, fwd, bwd, from_left, from_right,
    out, gq, gk, gv, heads, part, rep, *scratch,
):
    @pl.when(pl.program_id(0) == 0)
    def _():
        mark_repeats(ids, rep)

    each = len(scratch) // PER_STEP
    tiles = []
    for lt in range(PER_STEP):
        ls = slice(lt * LANES, (lt + 1) * LANES)
        tables = slice(lt * PER_TILE, (lt + 1) * PER_TILE)
        refs = [ref.at[:, ls] for ref in (q, k, v, g)]
        refs += [fwd.at[tables], bwd.at[tables]]
        refs += [ref.at[:, ls] for ref in (from_left, from_right, out, gq, gk, gv, heads)]
        refs += [part.at[pl.program_id(0) * PER_STEP + lt]]
        own = scratch[lt * each : (lt + 1) * each]
        tiles.append(Tile(refs, taps_ref[:, :, ls], skip_ref[:, ls], rep, own))
    together(tiles[0].activations())
    for n, tile in enumerate(tiles):
        following = tiles[n + 1 : n + 2]
        if n == 0:
            together(tile.forward_products(), *[t.activations() for t in following])
        together(tile.backward_products(), tile.query_side())
        together(tile.pair_products(), tile.key_value_side())
        together(
            tile.diagonals(), *[t.forward_products() for t in following], tile.finish()
        )


def back_kernel(grads, heads, taps_ref, result, frame):
    rows = grads.shape[0]
    step = 64
    for lt in range(grads.shape[1] // LANES):
        ls = slice(lt * LANES, (lt + 1) * LANES)
        frame[:rows] = grads[:, ls].astype(F32)
        frame[rows:] = heads[:, ls].astype(F32)
        for r in range(0, rows, step):
            total = taps_ref[0, 0:1, ls] * frame[pl.ds(r, step)]
            for j in range(1, SHORT):
                total = total + taps_ref[0, j : j + 1, ls] * frame[pl.ds(r + j, step)]
            result[r : r + step, ls] = total.astype(BF16)


def params(limit=60):
    return pltpu.CompilerParams(
        dimension_semantics=("arbitrary",), vmem_limit_bytes=limit * MIB
    )


def columns(rows, width):
    return pl.BlockSpec((rows, width), lambda i: (0, i))


def fixed(shape):
    return pl.BlockSpec(shape, lambda i: (0,) * len(shape))


def along_tile(count, width):
    return pl.BlockSpec((3, count, width), lambda i: (0, 0, i))


def make_edges(ids, q, k, v, g, taps):
    rows, channels = q.shape
    width = 1024
    first = pl.BlockSpec((TAPS, width), lambda i: (0, i))
    last = pl.BlockSpec((TAPS, width), lambda i: (rows // TAPS - 1, i))
    ahead = pl.BlockSpec((EDGE, width), lambda i: ((rows - TAPS) // EDGE - 1, i))
    tail = pl.BlockSpec((EDGE, width), lambda i: (rows // EDGE - 1, i))
    return pl.pallas_call(
        edges_kernel,
        grid=(channels // width,),
        in_specs=[pl.BlockSpec(memory_space=pltpu.SMEM), first, first, ahead, last, ahead, last]
        + [tail, along_tile(SHORT, width)],
        out_specs=[columns(TAPS + 2 * EDGE, width), columns(TAPS + 2 * EDGE, width)],
        out_shape=[
            jax.ShapeDtypeStruct((TAPS + 2 * EDGE, channels), BF16),
            jax.ShapeDtypeStruct((TAPS + 2 * EDGE, channels), BF16),
        ],
        scratch_shapes=[
            pltpu.VMEM((TAPS + EDGE, LANES), F32),
            pltpu.VMEM((TAPS + EDGE, LANES), F32),
            pltpu.VMEM((TAPS, LANES), F32),
            pltpu.VMEM((rows, LANES), F32),
        ],
        compiler_params=params(),
        name="edges",
    )(ids, q, g, k, k, v, v, q, taps)


def make_tables(long_filter, skip):
    groups = long_filter.shape[0]
    wide = pl.BlockSpec((PER_TILE, TAPS, 2 * TAPS), lambda i: (i, 0, 0))
    return pl.pallas_call(
        tables_kernel,
        grid=(groups // PER_TILE,),
        in_specs=[fixed(long_filter.shape), fixed(skip.shape)],
        out_specs=[wide, wide, fixed(skip.shape)],
        out_shape=[jax.ShapeDtypeStruct((groups, TAPS, 2 * TAPS), BF16)] * 2
        + [jax.ShapeDtypeStruct(skip.shape, F32)],
        scratch_shapes=[pltpu.VMEM((groups, TAPS), F32)] * 2,
        compiler_params=params(),
        cost_estimate=pl.CostEstimate(
            flops=0, bytes_accessed=32 * groups * TAPS * TAPS, transcendentals=0
        ),
        name="tables",
    )(long_filter, skip)


def make_main(ids, q, k, v, g, taps, skip, fwd, bwd, from_left, from_right):
    rows, channels = q.shape
    tiles = channels // LANES
    wide = pl.BlockSpec((PER_STEP * PER_TILE, TAPS, 2 * TAPS), lambda i: (i, 0, 0))
    big = jax.ShapeDtypeStruct((rows, channels), BF16)
    return pl.pallas_call(
        main_kernel,
        grid=(tiles // PER_STEP,),
        in_specs=[pl.BlockSpec(memory_space=pltpu.SMEM)]
        + [columns(rows, WIDE)] * 4
        + [along_tile(SHORT, WIDE), columns(1, WIDE), wide, wide]
        + [columns(from_left.shape[0], WIDE), columns(from_right.shape[0], WIDE)],
        out_specs=[columns(rows, WIDE)] * 4
        + [columns(3 * EDGE, WIDE), pl.BlockSpec(memory_space=pltpu.VMEM)],
        out_shape=[big] * 4
        + [
            jax.ShapeDtypeStruct((3 * EDGE, channels), BF16),
            pltpu.VMEM((tiles, PART_ROWS, LANES), F32),
        ],
        scratch_shapes=[pltpu.VMEM((rows, LANES), F32)]
        + PER_STEP
        * [
            pltpu.VMEM((rows + 2 * EDGE, LANES), F32),
            pltpu.VMEM((rows + EDGE, LANES), F32),
            pltpu.VMEM((rows + EDGE, LANES), F32),
            pltpu.VMEM((rows + TAPS, LANES), BF16),
            pltpu.VMEM((rows + TAPS, LANES), BF16),
            pltpu.VMEM((rows, LANES), F32),
            pltpu.VMEM((rows, LANES), F32),
            pltpu.VMEM((rows, LANES), F32),
            pltpu.VMEM((PER_TILE * TAPS, 2 * TAPS), F32),
            pltpu.VMEM((PER_TILE * TAPS, 2 * TAPS), F32),
            pltpu.VMEM((PER_TILE * TAPS, 2 * TAPS), F32),
            pltpu.VMEM((PER_TILE * 8, LANES), F32),
        ],
        compiler_params=params(),
        name="main",
    )(ids, q, k, v, g, taps, skip, fwd, bwd, from_left, from_right)


def make_back(which, grads, heads, taps):
    rows, channels = grads.shape
    width = 1024
    return pl.pallas_call(
        back_kernel,
        grid=(channels // width,),
        in_specs=[
            columns(rows, width),
            pl.BlockSpec((EDGE, width), lambda i: (which, i)),
            pl.BlockSpec((1, SHORT, width), lambda i: (which, 0, i)),
        ],
        out_specs=columns(rows, width),
        out_shape=jax.ShapeDtypeStruct((rows, channels), BF16),
        scratch_shapes=[pltpu.VMEM((rows + EDGE, LANES), F32)],
        compiler_params=params(),
        cost_estimate=pl.CostEstimate(
            flops=14 * rows * channels, bytes_accessed=8 * rows * channels, transcendentals=0
        ),
        name="back",
    )(grads, heads, taps)


def last_kernel(scale, which, half, other, long_grad, skip_grad, short_grad):
    mine = which[0]
    tiles = 2 * half.shape[0] // PART_ROWS
    for tile in range(tiles):
        side, at = divmod(tile, tiles // 2)
        rows = slice(at * PART_ROWS, (at + 1) * PART_ROWS)
        both = jnp.where(mine == side, half[rows], other[rows]) * scale
        ls = slice(tile * LANES, (tile + 1) * LANES)
        long_grad[tile * PER_TILE : (tile + 1) * PER_TILE] = both[:PER_TILE]
        for i in range(3):
            first = PER_TILE + i * SHORT
            short_grad[i, :, ls] = both[first : first + SHORT]
        skip_grad[ls] = both[PER_TILE + 3 * SHORT]


def make_last(half, other, which, scale):
    tiles = 2 * half.shape[0] // PART_ROWS
    channels = tiles * LANES
    return pl.pallas_call(
        functools.partial(last_kernel, scale),
        in_specs=[pl.BlockSpec(memory_space=pltpu.SMEM)]
        + [pl.BlockSpec(memory_space=pltpu.VMEM)] * 2,
        out_specs=[pl.BlockSpec(memory_space=pltpu.VMEM)] * 3,
        out_shape=[
            jax.ShapeDtypeStruct((tiles * PER_TILE, TAPS), F32),
            jax.ShapeDtypeStruct((channels,), F32),
            jax.ShapeDtypeStruct((3, SHORT, channels), F32),
        ],
        compiler_params=pltpu.CompilerParams(vmem_limit_bytes=4 * MIB),
        name="last",
    )(which.reshape(1).astype(jnp.int32), half, other)


def from_behind(value, steps):
    count = lax.axis_size("seg") * lax.axis_size("ctx")
    first, last = max(0, -steps), min(count, count - steps)
    return lax.ppermute(value, AXES, [(s, s + steps) for s in range(first, last)])


def swap(value, mask):
    count = lax.axis_size("seg") * lax.axis_size("ctx")
    return lax.ppermute(value, AXES, [(s, s ^ mask) for s in range(count)])


def joined(value, masks):
    got = [value] + [swap(value, mask) for mask in masks]
    while len(got) > 1:
        got = [one + other for one, other in zip(got[::2], got[1::2])]
    return got[0]


def ring_masks(size):
    masks = []
    span = 1
    while span < size:
        masks.append(span if 2 * span < size or size == 2 else span + span // 2)
        span *= 2
    return masks


def ring_steps(size):
    masks = ring_masks(size)
    return [(1, 2, 3)] + [(m,) for m in masks[2:]] if len(masks) > 1 else [(m,) for m in masks]


def total_over_all(value, work):
    ctx = lax.axis_size("ctx")
    seg = lax.axis_size("seg")
    me = lax.axis_index("seg") * ctx + lax.axis_index("ctx")
    cores = 2
    along = 1
    while along * along * cores < seg:
        along *= 2
    halving = [ctx, cores * ctx]
    x_unit, y_unit = cores * ctx, cores * ctx * along
    doubling = [(x_unit * m,) for m in ring_masks(along) if x_unit * m not in halving]
    doubling += [tuple(y_unit * m for m in step) for step in ring_steps(seg // (cores * along))]
    doubling += ring_steps(ctx)
    mine = []
    done = []
    pending = list(work)
    for mask in halving:
        half = value.shape[0] // 2
        high = ((me // mask) % 2) == 1
        if mask != ctx:
            high = high ^ (((me // (2 * mask)) % 2) == 1)
        low_part, high_part = value[:half], value[half:]
        mine.append(high)
        got = swap(jnp.where(high, low_part, high_part), mask)
        value = jnp.where(high, high_part, low_part) + got
    for n, masks in enumerate(doubling):
        job = pending.pop(0) if pending and n >= 1 else None
        if job is None:
            value = joined(value, masks)
            continue
        run, inputs = job
        value, inputs = lax.optimization_barrier((value, inputs))
        value, result = lax.optimization_barrier((joined(value, masks), run(*inputs)))
        done.append(result)
    done += [run(*inputs) for run, inputs in pending]
    for mask, high in zip(halving[:0:-1], mine[:0:-1]):
        got = swap(value, mask)
        value = jnp.where(
            high, jnp.concatenate([got, value]), jnp.concatenate([value, got])
        )
    return value, swap(value, halving[0]), mine[0], done


def per_device(
    token_ids, query_in, key_in, value_in, short_filters, long_filter, skip_gain, out_grad
):
    length, channels = query_in.shape
    tiles = channels // LANES
    to_right, to_left = make_edges(
        token_ids, query_in, key_in, value_in, out_grad, short_filters
    )
    from_left = from_behind(to_right, 1)
    from_right = from_behind(to_left, -1)
    fwd, bwd, skip = make_tables(long_filter, skip_gain.reshape(1, channels))
    out, gq, gk, gv, heads, part = make_main(
        token_ids, query_in, key_in, value_in, out_grad, short_filters,
        skip, fwd, bwd, from_left, from_right,
    )
    next_heads = from_behind(heads, -1)
    jobs = [
        (functools.partial(make_back, i), (grads, next_heads, short_filters))
        for i, grads in enumerate((gq, gk, gv))
    ]
    half, other, which, (grad_query, grad_key, grad_value) = total_over_all(
        part.reshape(tiles * PART_ROWS, LANES), jobs
    )
    norm_scale = float(length * lax.axis_size("seg") * lax.axis_size("ctx")) ** (-0.5)
    grad_long, grad_skip, grad_short = make_last(half, other, which, norm_scale)
    return out, grad_query, grad_key, grad_value, grad_long, grad_skip, grad_short


def solution(mesh):
    sharded = P(("seg", "ctx"), None)
    return jax.shard_map(
        per_device,
        mesh=mesh,
        in_specs=(P(("seg", "ctx")), sharded, sharded, sharded, P(), P(), P(), sharded),
        out_specs=(sharded, sharded, sharded, sharded, P(), P(), P()),
        check_vma=False,
    )
```
